512 devices in a mesh: ep: 128 (over z, y, core), dp: 4 (over x).
Axes of the slice: x: 4, y: 4, z: 16, core: 2. Of those that a mesh axis runs over, the one named last changes fastest.
Arguments:
- out_grads: bfloat16 [65536, 2048], P(('ep', 'dp')), may hold values from -40 to 40
- hidden_acts: bfloat16 [65536, 512], P(('ep', 'dp')), may hold values from -20 to 20
- routing: int32 [65536, 1], P(('ep', 'dp')), may hold values from 0 to 95, as said below
- replica_pick: int32 [65536], P(('ep', 'dp')), may hold values from 0 to 3
- master_weights: float32 [128, 2048, 512], P('ep', 'dp'), may hold values from -0.25 to 0.25
- current_slots: int32 [128], replicated, may hold values from 0 to 95, as said below
- next_slots: int32 [128], replicated, may hold values from 0 to 95, as said below
Outputs:
- input_grads: float32 [65536, 512], P(('ep', 'dp'))
- moved_weights: float32 [128, 2048, 512], P('ep', 'dp')
- moved_updates: float32 [128, 2048, 512], P('ep', 'dp')
The draws below stay inside these ranges and needn't reach their ends.
Inputs may be any that keep to these rules, and one draw needn't show every extreme that they name: `routing`: the rows of one device name each expert at most 2 times; the experts held by two slots now are named exactly 2 times by the rows of every device. `current_slots`: every expert below 96 is held by one or two slots. `next_slots`: every expert below 96 is held by at least one slot.
All inputs are finite; a program needn't handle non-finite values.
Results may differ from the reference program's by a relative error of at most 0.0029.
Values may be sent and summed in bfloat16 or wider, within the bound.
A program may use at most 64 MiB of HBM per device.

```python
import jax
import jax.numpy as jnp
from jax import lax

D = 2048
F = 512
TOK_DEV = 128
NS_STEPS = 2
EXPERTS = 96
CAP = 2
TOKENS = 65536
N_EP = 128
N_DP = 4


def draw_out_grads(key, part):
    salted = jax.random.fold_in(key, 11)
    noise_key, jitter_key = jax.random.split(salted, 2)
    noise = jnp.clip(jax.random.normal(noise_key, (TOKENS, D), jnp.float32), -4.0, 4.0)
    jitter = jax.random.uniform(jitter_key, (D,), jnp.float32)
    exponent = jnp.arange(D, dtype=jnp.float32) / D - 0.5 + 0.2 * (jitter - 0.5)
    scales = 10.0 ** exponent
    return (scales[None, :] * noise).astype(jnp.bfloat16)


def draw_hidden_acts(key, part):
    salted = jax.random.fold_in(key, 23)
    noise_key, scale_key = jax.random.split(salted)
    noise = jnp.clip(jax.random.normal(noise_key, (TOKENS, F), jnp.float32), -4.0, 4.0)
    scales = 10.0 ** (jax.random.uniform(scale_key, (F,), jnp.float32) - 0.5)
    return (scales[None, :] * noise).astype(jnp.bfloat16)


def expert_order(key):
    return jax.random.permutation(jax.random.fold_in(key, 5), jnp.arange(EXPERTS, dtype=jnp.int32))


def draw_routing(key, part):
    order = expert_order(key)
    hot_count = N_EP - EXPERTS
    hot_rows = jnp.repeat(order[:hot_count], CAP)
    cold_pool = jnp.repeat(order[hot_count:], CAP - 1)
    cold_take = TOK_DEV - hot_count * CAP
    salted = jax.random.fold_in(key, 61)

    def one_device(index):
        device_key = jax.random.fold_in(salted, index)
        picked = jax.random.permutation(jax.random.fold_in(device_key, 1), cold_pool)[:cold_take]
        rows = jnp.concatenate([hot_rows, picked])
        return jax.random.permutation(jax.random.fold_in(device_key, 2), rows)
    table = jax.vmap(one_device)(jnp.arange(TOKENS // TOK_DEV, dtype=jnp.int32))
    return table.reshape(TOKENS, 1).astype(jnp.int32)


def draw_current_slots(key, part):
    order = expert_order(key)
    ordinal = jnp.arange(N_EP, dtype=jnp.int32)
    extra = order[jnp.clip(ordinal - EXPERTS, 0, N_EP - EXPERTS - 1)]
    filled = jnp.where(ordinal < EXPERTS, ordinal, extra)
    return jax.random.permutation(jax.random.fold_in(key, 31), filled)


def draw_next_slots(key, part):
    order = expert_order(key)
    salted = jax.random.fold_in(key, 47)
    first, second = jax.random.split(salted)
    ordinal = jnp.arange(N_EP, dtype=jnp.int32)
    picks = jax.random.randint(first, (N_EP,), 0, N_EP - EXPERTS, dtype=jnp.int32)
    extra = order[picks]
    filled = jnp.where(ordinal < EXPERTS, ordinal, extra)
    return jax.random.permutation(second, filled)


def touch_ends(result, own_key, low, largest):
    longest = result.shape.index(max(result.shape))
    spots = []
    for shift in (0, 1):
        where = [jax.random.randint(jax.random.fold_in(own_key, axis), (), 0, length) for axis, length in enumerate(result.shape)]
        where[longest] = (where[longest] + shift) % result.shape[longest]
        spots.append(tuple(where))
    return result.at[spots[0]].set(low).at[spots[1]].set(largest)


def block_levels(own_key, dims, pieces, low, largest):
    def one(dim, blocks):
        draws = jax.random.uniform(jax.random.fold_in(jax.random.fold_in(own_key, 6), dim), (blocks,), jnp.float32, low / len(pieces), largest / len(pieces))
        return jnp.repeat(jnp.exp(draws), dims[dim] // blocks).reshape((-1,) + (1,) * (len(dims) - dim - 1))

    gain = one(*pieces[0])
    for cut in pieces[1:]:
        gain = gain * one(*cut)
    return gain


def bell_draw(rng, dims, deviation, bound, shards=(), kind=jnp.bfloat16):
    level = block_levels(rng, dims, shards, -0.22, 0.18) if shards else 1.0
    drawn = jax.random.normal(rng, dims, jnp.float32) * deviation * level
    return jnp.minimum(jnp.maximum(drawn, -bound), bound).astype(kind)


def setup_inputs(seed: int = 0) -> dict:
    key_list = jax.random.split(jax.random.key(seed), 8)
    out_grads = draw_out_grads(jax.random.fold_in(key_list[7], 71), 0)
    hidden_acts = draw_hidden_acts(jax.random.fold_in(key_list[7], 71), 0)
    routing = draw_routing(jax.random.fold_in(key_list[7], 71), 0)
    replica_pick = touch_ends(jax.random.randint(key_list[3], (TOKENS,), 0, 4), jax.random.fold_in(key_list[3], 1), 0, 3).astype(jnp.int32)
    master_weights = bell_draw(key_list[4], (N_EP, D, F), F ** -0.5, 0.25, ((0, 128), (1, 4)), jnp.float32)
    current_slots = draw_current_slots(jax.random.fold_in(key_list[7], 71), 0)
    next_slots = draw_next_slots(jax.random.fold_in(key_list[7], 71), 0)
    return {"out_grads": out_grads, "hidden_acts": hidden_acts, "routing": routing, "replica_pick": replica_pick, "master_weights": master_weights, "current_slots": current_slots, "next_slots": next_slots}


POLY_FIRST = 3.4445
POLY_SECOND = -4.775
POLY_THIRD = 2.0315
LEARNING_RATE = 0.02
UPDATE_SCALE = 0.2
EPSILON = 1e-07
PRECISE = lax.Precision.HIGHEST

def slot_ranks(placement):
    number = placement.shape[0]
    matching = placement[:, None] == placement[None, :]
    earlier = jnp.arange(number, dtype=jnp.int32)[None, :] < jnp.arange(number, dtype=jnp.int32)[:, None]
    return lax.optimization_barrier(jnp.sum(matching & earlier, axis=1)).astype(jnp.int32)

def choose_slots(placement, rankings, experts_named, wanted_index):
    holders = placement[None, :] == experts_named[:, None]
    totals = lax.optimization_barrier(jnp.sum(holders, axis=1)).astype(jnp.int32)
    wanted = jnp.remainder(wanted_index, totals)
    chosen = holders & (rankings[None, :] == wanted[:, None])
    ordinal = jnp.arange(placement.shape[0], dtype=jnp.int32)[None, :]
    return lax.optimization_barrier(jnp.sum(jnp.where(chosen, ordinal, 0), axis=1)).astype(jnp.int32)

def orthogonalize(grad):
    normed = grad / (jnp.sqrt(jnp.sum(grad * grad)) + EPSILON)
    for iteration in range(NS_STEPS):
        gram_now = jnp.dot(normed.T, normed, precision=PRECISE)
        polynomial = POLY_SECOND * gram_now + POLY_THIRD * jnp.dot(gram_now, gram_now, precision=PRECISE)
        normed = POLY_FIRST * normed + jnp.dot(normed, polynomial, precision=PRECISE)
    return UPDATE_SCALE * D ** 0.5 * normed

def reference(out_grads, hidden_acts, routing, replica_pick, master_weights, current_slots, next_slots):
    rankings = slot_ranks(current_slots)
    slot_of_row = choose_slots(current_slots, rankings, routing[:, 0], replica_pick)
    devices = TOKENS // TOK_DEV
    onehot = (slot_of_row.reshape(devices, TOK_DEV)[:, :, None] == jnp.arange(N_EP, dtype=jnp.int32)[None, None, :]).astype(jnp.int32)
    position = lax.optimization_barrier(jnp.sum(onehot * (jnp.cumsum(onehot, axis=1) - 1), axis=2)).reshape(-1).astype(jnp.int32)
    row_ids = jnp.arange(TOKENS, dtype=jnp.int32)
    device_of_row = row_ids // TOK_DEV
    source_ep = device_of_row // N_DP
    group_of_row = device_of_row % N_DP
    within = (group_of_row * (N_EP * CAP) + source_ep * CAP + position).astype(jnp.int32)
    inverse = jnp.full((N_EP, N_DP * N_EP * CAP), TOKENS, jnp.int32).at[slot_of_row, within].set(row_ids)
    grads_padded = jnp.concatenate([out_grads, jnp.zeros((1, D), out_grads.dtype)], axis=0)
    acts_padded = jnp.concatenate([hidden_acts, jnp.zeros((1, F), hidden_acts.dtype)], axis=0)

    def per_slot(operands):
        index, weight = operands
        rows_grads = grads_padded[index]
        rows_acts = acts_padded[index]
        back = jnp.dot(rows_grads, weight.astype(jnp.bfloat16), preferred_element_type=jnp.float32)

        def group_partial(pair):
            part_grads, part_acts = pair
            return jnp.dot(part_grads.T, part_acts, preferred_element_type=jnp.float32)
        partials = lax.map(group_partial, (rows_grads.reshape(N_DP, -1, D), rows_acts.reshape(N_DP, -1, F)))
        return (back, lax.optimization_barrier(jnp.sum(partials, axis=0)))
    backs, slot_grads = lax.map(per_slot, (inverse, master_weights))
    input_grads = backs[slot_of_row, within]
    expert_grads = jax.ops.segment_sum(slot_grads, current_slots, num_segments=EXPERTS)
    updates = lax.map(orthogonalize, expert_grads)
    experts_all = jnp.arange(EXPERTS, dtype=jnp.int32)
    homes = choose_slots(current_slots, rankings, experts_all, jnp.zeros_like(experts_all))
    fresh = master_weights[homes] - LEARNING_RATE * updates
    return (input_grads, fresh[next_slots], updates[next_slots])
```

```python
import jax
import jax.numpy as jnp
from jax import lax
from jax.sharding import PartitionSpec as P

POLY_FIRST = 3.4445
POLY_SECOND = -4.775
POLY_THIRD = 2.0315
LEARNING_RATE = 0.02
UPDATE_SCALE = 0.2
EPSILON = 1e-07
PRECISE = lax.Precision.HIGHEST
BF16 = jnp.bfloat16
F32 = jnp.float32


def slot_ranks(placement):
    number = placement.shape[0]
    ordinal = jnp.arange(number, dtype=jnp.int32)
    matching = placement[:, None] == placement[None, :]
    earlier = ordinal[None, :] < ordinal[:, None]
    return jnp.sum(matching & earlier, axis=1)


def pick(onehot, values):
    return jnp.dot(onehot.astype(BF16), values, preferred_element_type=BF16)


def exchange(array, axis):
    return lax.all_to_all(array, axis, split_axis=0, concat_axis=0, tiled=True)


def per_device(
    out_grads, hidden_acts, routing, replica_pick, master_weights, current_slots, next_slots
):
    rows, width = out_grads.shape
    hidden = hidden_acts.shape[1]
    n_ep = lax.axis_size("ep")
    n_dp = lax.axis_size("dp")
    part = width // n_dp
    local_master = master_weights[0]
    piece = part // n_ep

    pieces = exchange(local_master.astype(BF16).reshape(n_ep, piece * hidden), "ep")

    rank_now = slot_ranks(current_slots)
    rank_next = slot_ranks(next_slots)
    named = routing[:, 0]
    named_by = named[:, None] == current_slots[None, :]
    holders = jnp.sum(named_by, axis=1)
    rank_of_row = jnp.remainder(replica_pick, holders)
    ordinal = jnp.arange(rows, dtype=jnp.int32)
    twin = (named[:, None] == named[None, :]) & (ordinal[None, :] < ordinal[:, None])
    place = jnp.sum(twin, axis=1)
    places = jnp.arange(2, dtype=jnp.int32)
    wants = next_slots[:, None] == named[None, :]
    to_slot = wants[:, None, :] & (place[None, None, :] == places[None, :, None])
    to_slot = to_slot.reshape(2 * n_ep, rows)
    back = (wants & (rank_next == 0)[:, None])[:, None, :] & (
        place[None, None, :] == places[None, :, None]
    )
    back = back.reshape(2 * n_ep, rows)

    sent_grads = pick(to_slot, out_grads).reshape(2 * n_ep, n_dp, part).transpose(1, 0, 2)
    sent_grads = exchange(sent_grads, "dp").reshape(n_dp, n_ep, 2, part).transpose(1, 0, 2, 3)
    flags = jnp.broadcast_to(rank_of_row[:, None].astype(BF16), (rows, 128))
    acts_flags = jnp.concatenate([hidden_acts, flags], axis=1)
    sent_acts = pick(to_slot, acts_flags).reshape(n_ep, 2, hidden + 128)
    got_grads = exchange(sent_grads, "ep")
    got_acts = exchange(sent_acts, "ep")
    rows_grads = got_grads.transpose(1, 0, 2, 3).reshape(n_dp * n_ep * 2, part)
    gathered = lax.all_gather(got_acts.reshape(n_ep * 2, -1), "dp", axis=0, tiled=True)
    rows_acts = gathered[:, :hidden]
    rows_second = gathered[:, hidden : hidden + 1] != 0

    match = next_slots[:, None] == current_slots[None, :]
    first = match & (rank_now == 0)[None, :]
    second = match & (rank_now == 1)[None, :]
    both = jnp.stack([first, second], axis=1).reshape(2 * n_ep, n_ep)
    moved = exchange(pick(both, pieces).reshape(n_ep, 2, piece * hidden), "ep")
    moved = moved.reshape(n_ep, 2, piece, hidden).transpose(1, 0, 2, 3).reshape(2, part, hidden)

    grad = lax.dot_general(
        rows_grads, rows_acts, (((0,), (0,)), ((), ())), preferred_element_type=F32
    )
    gram = lax.psum(
        lax.dot_general(grad, grad, (((0,), (0,)), ((), ())), precision=PRECISE), "dp"
    )
    eye = jnp.eye(hidden, dtype=F32)
    scale = 1.0 / (jnp.sqrt(jnp.sum(gram * eye)) + EPSILON)
    a1 = gram * scale * scale
    q1 = (
        POLY_FIRST * eye
        + POLY_SECOND * a1
        + POLY_THIRD * jnp.dot(a1, a1, precision=PRECISE)
    )
    a2 = jnp.dot(jnp.dot(q1, a1, precision=PRECISE), q1, precision=PRECISE)
    q2 = (
        POLY_FIRST * eye
        + POLY_SECOND * a2
        + POLY_THIRD * jnp.dot(a2, a2, precision=PRECISE)
    )
    turn = jnp.dot(q1, q2, precision=PRECISE)
    update = jnp.dot(grad * (UPDATE_SCALE * width**0.5 * scale), turn, precision=PRECISE)
    moved_weight = moved[0].astype(F32) - LEARNING_RATE * update

    zero = jnp.zeros_like(rows_grads)
    lhs = jnp.concatenate(
        [jnp.where(rows_second, zero, rows_grads), jnp.where(rows_second, rows_grads, zero)],
        axis=1,
    )
    partial = jnp.dot(lhs, moved.reshape(2 * part, hidden), preferred_element_type=F32)
    spread = exchange(partial.astype(BF16).reshape(n_dp, n_ep * 2, hidden), "dp")
    summed = jnp.sum(spread.astype(F32), axis=0).astype(BF16)
    returned = exchange(summed.reshape(n_ep, 2, hidden), "ep").reshape(2 * n_ep, hidden)
    input_grads = lax.dot_general(
        back.astype(BF16), returned, (((0,), (0,)), ((), ())), preferred_element_type=F32
    )
    return (input_grads, moved_weight[None], update[None])


def solution(mesh):
    placed = (
        P(("ep", "dp"), None),
        P(("ep", "dp"), None),
        P(("ep", "dp"), None),
        P(("ep", "dp")),
        P("ep", "dp", None),
        P(),
        P(),
    )
    return jax.shard_map(
        per_device,
        mesh=mesh,
        in_specs=placed,
        out_specs=(P(("ep", "dp"), None), P("ep", "dp", None), P("ep", "dp", None)),
        check_vma=False,
    )
```

```python
import jax
import jax.numpy as jnp
from jax import lax
from jax.experimental import pallas as pl
from jax.experimental.pallas import tpu as pltpu
from jax.sharding import PartitionSpec as P

POLY_FIRST = 3.4445
POLY_SECOND = -4.775
POLY_THIRD = 2.0315
LEARNING_RATE = 0.02
UPDATE_SCALE = 0.2
EPSILON = 1e-07
PRECISE = lax.Precision.HIGHEST
BF16 = jnp.bfloat16
F32 = jnp.float32
MESH = pl.DeviceIdType.MESH
N_EP = 128
N_DP = 4
N_Z = 16
N_YC = 8
ROWS = 2 * N_EP
WIDE = 512
FLAG = 128


def slot_ranks(placement):
    number = placement.shape[0]
    ordinal = jnp.arange(number, dtype=jnp.int32)
    matching = placement[:, None] == placement[None, :]
    earlier = ordinal[None, :] < ordinal[:, None]
    return jnp.sum(matching & earlier, axis=1)


def pick(onehot, values):
    return jnp.dot(onehot.astype(BF16), values, preferred_element_type=BF16)


def span(start, size):
    return pl.ds(pl.multiple_of(start, size), size)


def wait_bytes(ref, sem):
    pltpu.make_async_copy(ref, ref, sem).wait()


def greet(me, col):
    barrier = pltpu.get_barrier_semaphore()

    def along_ep(i, carry):
        pl.semaphore_signal(
            barrier, inc=1, device_id={"ep": lax.rem(me + i, N_EP)}, device_id_type=MESH
        )
        return carry

    lax.fori_loop(1, N_EP, along_ep, 0)
    for k in range(1, N_DP):
        pl.semaphore_signal(
            barrier, inc=1, device_id={"dp": lax.rem(col + k, N_DP)}, device_id_type=MESH
        )
    pl.semaphore_wait(barrier, N_EP - 1 + N_DP - 1)


def send(src, dst, sems, where):
    pltpu.make_async_remote_copy(
        src_ref=src,
        dst_ref=dst,
        send_sem=sems.at[0],
        recv_sem=sems.at[1],
        device_id=where,
        device_id_type=MESH,
    ).start()


def turn_rows(values, outer, inner):
    shape = (ROWS, ROWS)
    row = lax.broadcasted_iota(jnp.int32, shape, 0)
    column = lax.broadcasted_iota(jnp.int32, shape, 1)
    o = row // (2 * inner)
    i = lax.rem(row, 2 * inner) // 2
    p = lax.rem(row, 2)
    onehot = (column == i * (2 * outer) + o * 2 + p).astype(F32).astype(BF16)
    return jnp.dot(onehot, values, preferred_element_type=F32).astype(BF16)


def front_kernel(
    w_ref, og_ref, ha_ref, wp_ref, ogz_ref, hg_ref,
    ogx, ogy, ogp, hy, hp,
    w_sem, x_sem, y_sem, hy_sem, z_sem, hz_sem, hx_sem,
):
    me = lax.axis_index("ep")
    col = lax.axis_index("dp")
    z = me // N_YC
    yc = lax.rem(me, N_YC)
    greet(me, col)

    for k in range(1, N_DP):
        peer = lax.rem(col + k, N_DP)
        send(og_ref.at[:, span(peer * WIDE, WIDE)], ogx.at[col], x_sem, {"dp": peer})
    for k in range(1, N_YC):
        peer = lax.rem(yc + k, N_YC)
        send(
            ha_ref.at[span(peer * 32, 32), :], hy.at[span(yc * 32, 32), :], hy_sem,
            {"ep": z * N_YC + peer},
        )

    def spread(i, carry):
        t = lax.rem(me + i, N_EP)
        tz = t // N_YC
        ty = lax.rem(t, N_YC)
        half = ty // 4
        send(
            w_ref.at[span(tz * 32 + half * 16, 16), span(lax.rem(ty, 4) * 128, 128)],
            wp_ref.at[me], w_sem, {"ep": t},
        )
        return carry

    lax.fori_loop(1, N_EP, spread, 0)
    wp_ref[me] = w_ref[
        span(z * 32 + (yc // 4) * 16, 16), span(lax.rem(yc, 4) * 128, 128)
    ]

    hy[span(yc * 32, 32), :] = ha_ref[span(yc * 32, 32), :]
    wait_bytes(hy.at[pl.ds(0, 32 * (N_YC - 1)), :], hy_sem.at[1])
    hp[...] = turn_rows(hy[...], N_Z, N_YC)

    def acts_z(i, carry):
        peer = lax.rem(z + i, N_Z)
        send(
            hp.at[span(peer * 16, 16), :], hg_ref.at[col, span(z * 16, 16), :], hz_sem,
            {"ep": peer * N_YC + yc},
        )
        return carry

    lax.fori_loop(1, N_Z, acts_z, 0)
    hg_ref[col, span(z * 16, 16), :] = hp[span(z * 16, 16), :]

    ogx[col] = og_ref[:, span(col * WIDE, WIDE)]
    wait_bytes(ogx.at[pl.ds(0, N_DP - 1)], x_sem.at[1])
    for k in range(1, N_YC):
        peer = lax.rem(yc + k, N_YC)
        send(
            ogx.at[:, span(peer * 32, 32), :], ogy.at[:, span(yc * 32, 32), :], y_sem,
            {"ep": z * N_YC + peer},
        )
    ogy[:, span(yc * 32, 32), :] = ogx[:, span(yc * 32, 32), :]
    wait_bytes(ogy.at[:, pl.ds(0, 32 * (N_YC - 1)), :], y_sem.at[1])
    for g in range(N_DP):
        ogp[g] = turn_rows(ogy[g], N_Z, N_YC)

    def grads_z(i, carry):
        peer = lax.rem(z + i, N_Z)
        send(
            ogp.at[:, span(peer * 16, 16), :], ogz_ref.at[:, span(z * 16, 16), :], z_sem,
            {"ep": peer * N_YC + yc},
        )
        return carry

    lax.fori_loop(1, N_Z, grads_z, 0)
    ogz_ref[:, span(z * 16, 16), :] = ogp[:, span(z * 16, 16), :]

    wait_bytes(hp.at[pl.ds(0, 16 * (N_Z - 1)), :], hz_sem.at[1])
    for k in range(1, N_DP):
        peer = lax.rem(col + k, N_DP)
        send(hg_ref.at[col], hg_ref.at[col], hx_sem, {"dp": peer})

    wait_bytes(hg_ref.at[pl.ds(0, N_DP - 1)], hx_sem.at[1])
    wait_bytes(wp_ref.at[pl.ds(0, N_EP - 1)], w_sem.at[1])
    wait_bytes(ogz_ref.at[:, pl.ds(0, 16 * (N_Z - 1)), :], z_sem.at[1])
    wait_bytes(hy.at[pl.ds(0, 32 * (N_YC - 1)), :], hy_sem.at[0])
    wait_bytes(ogx.at[pl.ds(0, N_DP - 1)], x_sem.at[0])
    wait_bytes(hp.at[pl.ds(0, 16 * (N_Z - 1)), :], hz_sem.at[0])
    wait_bytes(ogy.at[:, pl.ds(0, 32 * (N_YC - 1)), :], y_sem.at[0])
    wait_bytes(hg_ref.at[pl.ds(0, N_DP - 1)], hx_sem.at[0])
    wait_bytes(wp_ref.at[pl.ds(0, N_EP - 1)], w_sem.at[0])
    wait_bytes(ogz_ref.at[:, pl.ds(0, 16 * (N_Z - 1)), :], z_sem.at[0])


def exact(left, right):
    return jnp.dot(left, right, precision=PRECISE, preferred_element_type=F32)


def back_kernel(
    ws_ref, ogz_ref, hg_ref, ret_ref, upd_ref, mov_ref,
    w01, grad, gram, gram_got, poly, turn, part_send, part_got, total, sums, bz, bp,
    w_sem, g_sem, a_sem, p_sem, z_sem, y_sem,
):
    me = lax.axis_index("ep")
    col = lax.axis_index("dp")
    z = me // N_YC
    yc = lax.rem(me, N_YC)
    greet(me, col)
    my_rows = span(z * 32 + (yc // 4) * 16, 16)
    my_cols = span(lax.rem(yc, 4) * 128, 128)

    def hop(i, carry):
        t = lax.rem(me + i, N_EP)
        send(ws_ref.at[t], w01.at[:, my_rows, my_cols], w_sem, {"ep": t})
        return carry

    lax.fori_loop(1, N_EP, hop, 0)
    w01[:, my_rows, my_cols] = ws_ref[me]

    acts = hg_ref[:, :, :WIDE].reshape(N_DP * ROWS, WIDE)
    for c in range(0, WIDE, 256):
        grad[c : c + 256, :] = lax.dot_general(
            ogz_ref[:, :, c : c + 256].reshape(N_DP * ROWS, 256),
            acts,
            (((0,), (0,)), ((), ())),
            preferred_element_type=F32,
        )
    for c in range(0, WIDE, 128):
        gram[c : c + 128, :] = exact(grad[:, c : c + 128].T, grad[...])

    for k in range(1, N_DP):
        peer = lax.rem(col + k, N_DP)
        send(gram.at[span(peer * 128, 128), :], gram_got.at[k - 1], g_sem.at[k - 1], {"dp": peer})
    share = gram[span(col * 128, 128), :]
    for k in range(1, N_DP):
        wait_bytes(gram_got.at[k - 1], g_sem.at[k - 1, 1])
        share = share + gram_got[k - 1]
    for k in range(1, N_DP):
        wait_bytes(gram_got.at[k - 1], g_sem.at[k - 1, 0])
    poly[span(col * 128, 128), :] = share
    for k in range(1, N_DP):
        peer = lax.rem(col + k, N_DP)
        send(
            poly.at[span(col * 128, 128), :], poly.at[span(col * 128, 128), :], a_sem,
            {"dp": peer},
        )
    wait_bytes(gram_got, a_sem.at[1])
    wait_bytes(gram_got, a_sem.at[0])

    row = lax.broadcasted_iota(jnp.int32, (WIDE, WIDE), 0)
    column = lax.broadcasted_iota(jnp.int32, (WIDE, WIDE), 1)
    eye = (row == column).astype(F32)
    square = jnp.sum(poly[...] * eye, keepdims=True)
    scale = 1.0 / (jnp.sqrt(square) + EPSILON)
    a1 = poly[...] * scale * scale
    q1 = POLY_FIRST * eye + POLY_SECOND * a1 + POLY_THIRD * exact(a1, a1)
    a2 = exact(exact(q1, a1), q1)
    q2 = POLY_FIRST * eye + POLY_SECOND * a2 + POLY_THIRD * exact(a2, a2)
    turn[...] = exact(q1, q2) * (scale * (UPDATE_SCALE * (N_DP * WIDE) ** 0.5))
    upd_ref[...] = exact(grad[...], turn[...])

    wait_bytes(ws_ref.at[pl.ds(0, N_EP - 1)], w_sem.at[1])
    for k in (1, 2, 3, 0):
        g = lax.rem(col + k, N_DP)
        flag = jnp.concatenate([hg_ref[g, :, WIDE:]] * (WIDE // FLAG), axis=1).astype(F32)
        rows = ogz_ref[g].astype(F32)
        product = jnp.dot(
            (rows * (1.0 - flag)).astype(BF16), w01[0], preferred_element_type=F32
        ) + jnp.dot((rows * flag).astype(BF16), w01[1], preferred_element_type=F32)
        if k:
            part_send[k - 1] = product.astype(BF16)
            send(part_send.at[k - 1], part_got.at[k - 1], p_sem, {"dp": g})
        else:
            total[...] = product
    mov_ref[...] = w01[0].astype(F32) - LEARNING_RATE * upd_ref[...]
    wait_bytes(part_got, p_sem.at[1])
    sums[...] = (
        total[...]
        + part_got[0].astype(F32)
        + part_got[1].astype(F32)
        + part_got[2].astype(F32)
    ).astype(BF16)

    def home_z(i, carry):
        peer = lax.rem(z + i, N_Z)
        send(
            sums.at[span(peer * 16, 16), :], bz.at[span(z * 16, 16), :], z_sem,
            {"ep": peer * N_YC + yc},
        )
        return carry

    lax.fori_loop(1, N_Z, home_z, 0)
    bz[span(z * 16, 16), :] = sums[span(z * 16, 16), :]
    wait_bytes(bz.at[pl.ds(0, 16 * (N_Z - 1)), :], z_sem.at[1])
    bp[...] = turn_rows(bz[...], N_YC, N_Z)
    for k in range(1, N_YC):
        peer = lax.rem(yc + k, N_YC)
        send(
            bp.at[span(peer * 32, 32), :], ret_ref.at[span(yc * 32, 32), :], y_sem,
            {"ep": z * N_YC + peer},
        )
    ret_ref[span(yc * 32, 32), :] = bp[span(yc * 32, 32), :]
    wait_bytes(ret_ref.at[pl.ds(0, 32 * (N_YC - 1)), :], y_sem.at[1])
    wait_bytes(ret_ref.at[pl.ds(0, 32 * (N_YC - 1)), :], y_sem.at[0])
    wait_bytes(bz.at[pl.ds(0, 16 * (N_Z - 1)), :], z_sem.at[0])
    wait_bytes(part_got, p_sem.at[0])
    wait_bytes(ws_ref.at[pl.ds(0, N_EP - 1)], w_sem.at[0])


def call(kernel, outs, scratch, semaphores, collective_id, *args):
    vmem = pl.BlockSpec(memory_space=pltpu.VMEM)
    return pl.pallas_call(
        kernel,
        out_shape=[jax.ShapeDtypeStruct(*o) for o in outs],
        in_specs=[vmem] * len(args),
        out_specs=[vmem] * len(outs),
        scratch_shapes=[pltpu.VMEM(*s) for s in scratch]
        + [pltpu.SemaphoreType.DMA(s) for s in semaphores],
        compiler_params=pltpu.CompilerParams(
            collective_id=collective_id, has_side_effects=True, vmem_limit_bytes=48 * 2**20
        ),
    )(*args)


def per_device(
    out_grads, hidden_acts, routing, replica_pick, master_weights, current_slots, next_slots
):
    rows = out_grads.shape[0]

    rank_now = slot_ranks(current_slots)
    rank_next = slot_ranks(next_slots)
    named = routing[:, 0]
    holders = jnp.sum(named[:, None] == current_slots[None, :], axis=1)
    rank_of_row = jnp.remainder(replica_pick, holders)
    ordinal = jnp.arange(rows, dtype=jnp.int32)
    twin = (named[:, None] == named[None, :]) & (ordinal[None, :] < ordinal[:, None])
    place = jnp.sum(twin, axis=1)
    places = jnp.arange(2, dtype=jnp.int32)
    next_turned = next_slots.reshape(N_Z, N_YC).T.reshape(-1)
    rank_turned = rank_next.reshape(N_Z, N_YC).T.reshape(-1)
    wants = next_turned[:, None] == named[None, :]
    placed = place[None, None, :] == places[None, :, None]
    to_slot = (wants[:, None, :] & placed).reshape(ROWS, rows)
    back = ((wants & (rank_turned == 0)[:, None])[:, None, :] & placed).reshape(ROWS, rows)

    flags = jnp.broadcast_to(rank_of_row[:, None].astype(BF16), (rows, FLAG))
    acts_flags = jnp.concatenate([hidden_acts, flags], axis=1)
    pieces, rows_grads, rows_acts = call(
        front_kernel,
        [((N_EP, 16, 128), BF16), ((N_DP, ROWS, WIDE), BF16), ((N_DP, ROWS, WIDE + FLAG), BF16)],
        [((N_DP, ROWS, WIDE), BF16)] * 3 + [((ROWS, WIDE + FLAG), BF16)] * 2,
        [(2,)] * 7,
        0,
        master_weights[0].astype(BF16),
        pick(to_slot, out_grads),
        pick(to_slot, acts_flags),
    )

    match = next_slots[:, None] == current_slots[None, :]
    first = match & (rank_now == 0)[None, :]
    second = match & (rank_now == 1)[None, :]
    both = jnp.stack([first, second], axis=1).reshape(ROWS, N_EP)
    chosen = pick(both, pieces.reshape(N_EP, 16 * 128)).reshape(N_EP, 2, 16, 128)

    returned, update, moved_weight = call(
        back_kernel,
        [((ROWS, WIDE), BF16), ((WIDE, WIDE), F32), ((WIDE, WIDE), F32)],
        [
            ((2, WIDE, WIDE), BF16),
            ((WIDE, WIDE), F32),
            ((WIDE, WIDE), F32),
            ((3, 128, WIDE), F32),
            ((WIDE, WIDE), F32),
            ((WIDE, WIDE), F32),
            ((3, ROWS, WIDE), BF16),
            ((3, ROWS, WIDE), BF16),
            ((ROWS, WIDE), F32),
            ((ROWS, WIDE), BF16),
            ((ROWS, WIDE), BF16),
            ((ROWS, WIDE), BF16),
        ],
        [(2,), (3, 2), (2,), (2,), (2,), (2,)],
        1,
        chosen,
        rows_grads,
        rows_acts,
    )
    input_grads = lax.dot_general(
        back.astype(BF16), returned, (((0,), (0,)), ((), ())), preferred_element_type=F32
    )
    return (input_grads, moved_weight[None], update[None])


def solution(mesh):
    placed = (
        P(("ep", "dp"), None),
        P(("ep", "dp"), None),
        P(("ep", "dp"), None),
        P(("ep", "dp")),
        P("ep", "dp", None),
        P(),
        P(),
    )
    return jax.shard_map(
        per_device,
        mesh=mesh,
        in_specs=placed,
        out_specs=(P(("ep", "dp"), None), P("ep", "dp", None), P("ep", "dp", None)),
        check_vma=False,
    )
```

```python
import jax
import jax.numpy as jnp
from jax import lax
from jax.experimental import pallas as pl
from jax.experimental.pallas import tpu as pltpu
from jax.sharding import PartitionSpec as P

POLY_FIRST = 3.4445
POLY_SECOND = -4.775
POLY_THIRD = 2.0315
LEARNING_RATE = 0.02
UPDATE_SCALE = 0.2
EPSILON = 1e-07
PRECISE = lax.Precision.HIGHEST
BF16 = jnp.bfloat16
F32 = jnp.float32
MESH = pl.DeviceIdType.MESH
N_EP = 128
N_DP = 4
N_Z = 16
N_YC = 8
ROWS = 2 * N_EP
WIDE = 512
FLAG = 128
CHUNKS = 2
CHUNK = WIDE // CHUNKS


def span(start, size):
    return pl.ds(pl.multiple_of(start, size), size)


def wait_bytes(ref, sem):
    pltpu.make_async_copy(ref, ref, sem).wait()


def greet(z, yc, col):
    barrier = pltpu.get_barrier_semaphore()
    for k in range(1, N_Z):
        peer = lax.rem(z + k, N_Z) * N_YC + yc
        pl.semaphore_signal(barrier, inc=1, device_id={"ep": peer}, device_id_type=MESH)
    for k in range(1, N_YC):
        peer = z * N_YC + lax.rem(yc + k, N_YC)
        pl.semaphore_signal(barrier, inc=1, device_id={"ep": peer}, device_id_type=MESH)
    for k in range(1, N_DP):
        peer = lax.rem(col + k, N_DP)
        pl.semaphore_signal(barrier, inc=1, device_id={"dp": peer}, device_id_type=MESH)
    pl.semaphore_wait(barrier, N_Z - 1 + N_YC - 1 + N_DP - 1)


def send(src, dst, sems, where):
    pltpu.make_async_remote_copy(
        src_ref=src,
        dst_ref=dst,
        send_sem=sems.at[0],
        recv_sem=sems.at[1],
        device_id=where,
        device_id_type=MESH,
    ).start()


def turn_rows(values, outer, inner):
    shape = (ROWS, ROWS)
    row = lax.broadcasted_iota(jnp.int32, shape, 0)
    column = lax.broadcasted_iota(jnp.int32, shape, 1)
    o = row // (2 * inner)
    i = lax.rem(row, 2 * inner) // 2
    p = lax.rem(row, 2)
    onehot = (column == i * (2 * outer) + o * 2 + p).astype(F32).astype(BF16)
    return jnp.dot(onehot, values, preferred_element_type=F32).astype(BF16)


def exact(left, right):
    return jnp.dot(left, right, precision=PRECISE, preferred_element_type=F32)


def pick(onehot, values):
    return jnp.dot(onehot, values, preferred_element_type=F32).astype(BF16)


def iota(shape, dimension):
    return lax.broadcasted_iota(jnp.int32, shape, dimension)


def count(mask, axis):
    return jnp.sum(mask.astype(F32), axis=axis, keepdims=True)


def plan(named_ref, pick_ref, now_ref, next_ref):
    square = (N_EP, N_EP)
    upper, lower = iota(square, 0), iota(square, 1)

    def column(row):
        return jnp.sum(jnp.where(upper == lower, row, 0.0), axis=1, keepdims=True)

    named = named_ref[...].astype(F32)
    now = now_ref[...].astype(F32)
    later = next_ref[...].astype(F32)
    now_column = column(now)
    place = count((column(named) == named) & (upper < lower), 0)
    holders = count(now_column == named, 0)
    second = jnp.where(
        (holders == 2.0) & (lax.rem(pick_ref[...], 2) == 1), 1.0, 0.0
    )
    rank_now = count((now_column == now) & (lower < upper), 1)
    rank_next = count((column(later) == later) & (upper < lower), 0)
    turned = upper == lax.rem(lower, N_Z) * N_YC + lower // N_Z
    now_turned = jnp.sum(jnp.where(turned, now_column, 0.0), axis=0, keepdims=True)
    rank_turned = jnp.sum(jnp.where(turned, rank_now, 0.0), axis=0, keepdims=True)
    tall = (ROWS, N_EP)
    row, lane = iota(tall, 0), iota(tall, 1)
    own = lane == lax.rem(row // 2, N_Z) * N_YC + row // (2 * N_Z)
    wanted = jnp.sum(jnp.where(own, later, 0.0), axis=1, keepdims=True)
    leads = jnp.sum(jnp.where(own, rank_next, 0.0), axis=1, keepdims=True) == 0.0
    pair = lax.rem(row, 2).astype(F32)
    to_slot = jnp.where((wanted == named) & (place == pair), 1.0, 0.0)
    back = jnp.where(leads, to_slot, 0.0)
    flag = jnp.sum(to_slot * second, axis=1, keepdims=True)
    hop = jnp.where((wanted == now_turned) & (rank_turned == pair), 1.0, 0.0)
    return to_slot.astype(BF16), back.astype(BF16), flag, hop.astype(BF16)


def kernel(
    og_ref, ha_ref, named_ref, pick_ref, weight_ref, now_ref, next_ref,
    out_ref, mov_ref, upd_ref,
    wb, wz, wp, wide, chosen, pay, hop, w01,
    ogs, ogx, ogy, ogp, ogz, has, hy, hp, hg, back,
    lhs, grad, gram, gram_got, poly, turn,
    part_send, part_got, total, sums, bz, bp, ret,
    wz_sem, wy_sem, hopy_sem, hopz_sem, x_sem, y_sem, z_sem, hy_sem, hz_sem, hx_sem,
    g_sem, a_sem, p_sem, bz_sem, by_sem,
):
    me = lax.axis_index("ep")
    col = lax.axis_index("dp")
    z = me // N_YC
    yc = lax.rem(me, N_YC)

    def over_z(body):
        def step(k, carry):
            peer = lax.rem(z + k, N_Z)
            body(peer, {"ep": peer * N_YC + yc})
            return carry

        lax.fori_loop(1, N_Z, step, 0)

    def over_yc(body):
        def step(k, carry):
            peer = lax.rem(yc + k, N_YC)
            body(peer, {"ep": z * N_YC + peer})
            return carry

        lax.fori_loop(1, N_YC, step, 0)

    my16, my32z, my32y = span(z * 16, 16), span(z * 32, 32), span(yc * 32, 32)
    my_half, my_cols = span((yc // 4) * 16, 16), span(lax.rem(yc, 4) * 128, 128)

    greet(z, yc, col)

    wb[...] = weight_ref[...].astype(BF16)
    over_z(lambda peer, there: send(wb.at[span(peer * 32, 32), :], wz.at[z], wz_sem, there))
    wz[z] = wb[my32z, :]

    to_slot, leading, flag, hop_onehot = plan(named_ref, pick_ref, now_ref, next_ref)
    back[...] = leading
    ogs[...] = pick(to_slot, og_ref[...])
    for k in range(1, N_DP):
        peer = lax.rem(col + k, N_DP)
        send(ogs.at[:, span(peer * WIDE, WIDE)], ogx.at[col], x_sem, {"dp": peer})
    has[:, :WIDE] = pick(to_slot, ha_ref[...])
    has[:, WIDE:] = jnp.broadcast_to(flag, (ROWS, FLAG)).astype(BF16)
    over_yc(
        lambda peer, there: send(has.at[span(peer * 32, 32), :], hy.at[my32y, :], hy_sem, there)
    )
    hy[my32y, :] = has[my32y, :]
    ogx[col] = ogs[:, span(col * WIDE, WIDE)]

    wait_bytes(hy.at[pl.ds(0, 32 * (N_YC - 1)), :], hy_sem.at[1])
    hp[...] = turn_rows(hy[...], N_Z, N_YC)
    over_z(
        lambda peer, there: send(
            hp.at[span(peer * 16, 16), :], hg.at[col, my16, :], hz_sem, there
        )
    )
    hg[col, my16, :] = hp[my16, :]

    wait_bytes(ogx.at[pl.ds(0, N_DP - 1)], x_sem.at[1])
    over_yc(
        lambda peer, there: send(
            ogx.at[:, span(peer * 32, 32), :], ogy.at[:, my32y, :], y_sem, there
        )
    )
    ogy[:, my32y, :] = ogx[:, my32y, :]

    wait_bytes(wz.at[pl.ds(0, N_Z - 1)], wz_sem.at[1])
    over_yc(
        lambda peer, there: send(
            wz.at[:, span((peer // 4) * 16, 16), span(lax.rem(peer, 4) * 128, 128)],
            wp.at[yc], wy_sem, there,
        )
    )
    wp[yc] = wz[:, my_half, my_cols]

    wait_bytes(ogy.at[:, pl.ds(0, 32 * (N_YC - 1)), :], y_sem.at[1])
    for g in range(N_DP):
        ogp[g] = turn_rows(ogy[g], N_Z, N_YC)
    over_z(
        lambda peer, there: send(
            ogp.at[:, span(peer * 16, 16), :], ogz.at[:, my16, :], z_sem, there
        )
    )
    ogz[:, my16, :] = ogp[:, my16, :]

    wait_bytes(wp.at[pl.ds(0, N_YC - 1)], wy_sem.at[1])
    wide[...] = wp[...].reshape(N_EP * 16, 128).astype(F32)
    for j in range(16):
        piece = wide[pl.ds(j, N_EP, stride=16), :].astype(BF16)
        chosen[pl.ds(j, ROWS, stride=16), :] = jnp.dot(
            hop_onehot, piece, preferred_element_type=F32
        )
    pay[...] = chosen[...].astype(BF16).reshape(N_YC, N_Z, 2, 16, 128)
    over_yc(
        lambda peer, there: send(
            pay.at[peer], hop.at[:, :, my_half, my_cols], hopy_sem, there
        )
    )
    hop[:, :, my_half, my_cols] = pay[yc]

    wait_bytes(hp.at[pl.ds(0, 16 * (N_Z - 1)), :], hz_sem.at[1])
    for k in range(1, N_DP):
        peer = lax.rem(col + k, N_DP)
        send(hg.at[col], hg.at[col], hx_sem, {"dp": peer})

    wait_bytes(pay.at[pl.ds(0, N_YC - 1)], hopy_sem.at[1])
    over_z(lambda peer, there: send(hop.at[peer], w01.at[:, my32z, :], hopz_sem, there))
    w01[:, my32z, :] = hop[z]

    wait_bytes(hg.at[pl.ds(0, N_DP - 1)], hx_sem.at[1])
    wait_bytes(ogz.at[:, pl.ds(0, 16 * (N_Z - 1)), :], z_sem.at[1])
    acts = hg[:, :, :WIDE].reshape(N_DP * ROWS, WIDE)
    for c in range(0, WIDE, 256):
        grad[c : c + 256, :] = lax.dot_general(
            ogz[:, :, c : c + 256].reshape(N_DP * ROWS, 256),
            acts,
            (((0,), (0,)), ((), ())),
            preferred_element_type=F32,
        )
    for c in range(0, WIDE, 128):
        gram[c : c + 128, :] = exact(grad[:, c : c + 128].T, grad[...])

    for k in range(1, N_DP):
        peer = lax.rem(col + k, N_DP)
        send(gram.at[span(peer * 128, 128), :], gram_got.at[k - 1], g_sem.at[k - 1], {"dp": peer})
    for g in range(N_DP):
        second = jnp.concatenate([hg[g, :, WIDE:]] * (WIDE // FLAG), axis=1).astype(F32)
        rows = ogz[g].astype(F32)
        lhs[g, :, :WIDE] = (rows * (1.0 - second)).astype(BF16)
        lhs[g, :, WIDE:] = (rows * second).astype(BF16)
    share = gram[span(col * 128, 128), :]
    for k in range(1, N_DP):
        wait_bytes(gram_got.at[k - 1], g_sem.at[k - 1, 1])
        share = share + gram_got[k - 1]
    poly[span(col * 128, 128), :] = share
    for k in range(1, N_DP):
        peer = lax.rem(col + k, N_DP)
        send(
            poly.at[span(col * 128, 128), :], poly.at[span(col * 128, 128), :], a_sem,
            {"dp": peer},
        )
    for k in range(1, N_DP):
        wait_bytes(gram_got.at[k - 1], g_sem.at[k - 1, 0])
    wait_bytes(gram_got, a_sem.at[1])
    wait_bytes(gram_got, a_sem.at[0])

    eye = jnp.where(iota((WIDE, WIDE), 0) == iota((WIDE, WIDE), 1), 1.0, 0.0)
    square = jnp.sum(poly[...] * eye, keepdims=True)
    scale = 1.0 / (jnp.sqrt(square) + EPSILON)
    a1 = poly[...] * scale * scale
    q1 = POLY_FIRST * eye + POLY_SECOND * a1 + POLY_THIRD * exact(a1, a1)
    a2 = exact(exact(q1, a1), q1)
    q2 = POLY_FIRST * eye + POLY_SECOND * a2 + POLY_THIRD * exact(a2, a2)
    turn[...] = exact(q1, q2) * (scale * (UPDATE_SCALE * (N_DP * WIDE) ** 0.5))
    upd_ref[...] = exact(grad[...], turn[...])

    wait_bytes(hop.at[pl.ds(0, N_Z - 1)], hopz_sem.at[1])
    for c in range(CHUNKS):
        lanes = pl.ds(c * CHUNK, CHUNK)
        weight = w01[:, :, lanes].reshape(2 * WIDE, CHUNK)
        for k in (1, 2, 3, 0):
            g = lax.rem(col + k, N_DP)
            product = jnp.dot(lhs[g], weight, preferred_element_type=F32)
            if k:
                part_send[c, k - 1] = product.astype(BF16)
                send(part_send.at[c, k - 1], part_got.at[c, k - 1], p_sem.at[c], {"dp": g})
            else:
                total[c] = product
    for c in range(CHUNKS):
        wait_bytes(part_got.at[c], p_sem.at[c, 1])
        got = part_got[c].astype(F32)
        sums[c] = (total[c] + got[0] + got[1] + got[2]).astype(BF16)
        over_z(
            lambda peer, there: send(
                sums.at[c, span(peer * 16, 16), :], bz.at[c, my16, :], bz_sem.at[c], there
            )
        )
        bz[c, my16, :] = sums[c, my16, :]
    mov_ref[...] = w01[0].astype(F32) - LEARNING_RATE * upd_ref[...]
    for c in range(CHUNKS):
        wait_bytes(bz.at[c, pl.ds(0, 16 * (N_Z - 1)), :], bz_sem.at[c, 1])
        bp[c] = turn_rows(bz[c], N_YC, N_Z)
        over_yc(
            lambda peer, there: send(
                bp.at[c, span(peer * 32, 32), :], ret.at[c, my32y, :], by_sem.at[c], there
            )
        )
        ret[c, my32y, :] = bp[c, my32y, :]
    for c in range(CHUNKS):
        wait_bytes(ret.at[c, pl.ds(0, 32 * (N_YC - 1)), :], by_sem.at[c, 1])
        out_ref[:, pl.ds(c * CHUNK, CHUNK)] = lax.dot_general(
            back[...], ret[c], (((0,), (0,)), ((), ())), preferred_element_type=F32
        )

    for c in range(CHUNKS):
        wait_bytes(part_got.at[c], p_sem.at[c, 0])
        wait_bytes(bz.at[c, pl.ds(0, 16 * (N_Z - 1)), :], bz_sem.at[c, 0])
        wait_bytes(ret.at[c, pl.ds(0, 32 * (N_YC - 1)), :], by_sem.at[c, 0])
    wait_bytes(wz.at[pl.ds(0, N_Z - 1)], wz_sem.at[0])
    wait_bytes(wp.at[pl.ds(0, N_YC - 1)], wy_sem.at[0])
    wait_bytes(pay.at[pl.ds(0, N_YC - 1)], hopy_sem.at[0])
    wait_bytes(hop.at[pl.ds(0, N_Z - 1)], hopz_sem.at[0])
    wait_bytes(ogx.at[pl.ds(0, N_DP - 1)], x_sem.at[0])
    wait_bytes(ogy.at[:, pl.ds(0, 32 * (N_YC - 1)), :], y_sem.at[0])
    wait_bytes(ogz.at[:, pl.ds(0, 16 * (N_Z - 1)), :], z_sem.at[0])
    wait_bytes(hy.at[pl.ds(0, 32 * (N_YC - 1)), :], hy_sem.at[0])
    wait_bytes(hp.at[pl.ds(0, 16 * (N_Z - 1)), :], hz_sem.at[0])
    wait_bytes(hg.at[pl.ds(0, N_DP - 1)], hx_sem.at[0])


def call(kernel, outs, scratch, semaphores, collective_id, *args):
    vmem = pl.BlockSpec(memory_space=pltpu.VMEM)
    return pl.pallas_call(
        kernel,
        out_shape=[jax.ShapeDtypeStruct(*o) for o in outs],
        in_specs=[vmem] * len(args),
        out_specs=[vmem] * len(outs),
        scratch_shapes=[pltpu.VMEM(*s) for s in scratch]
        + [pltpu.SemaphoreType.DMA(s) for s in semaphores],
        compiler_params=pltpu.CompilerParams(
            collective_id=collective_id, has_side_effects=True, vmem_limit_bytes=48 * 2**20
        ),
    )(*args)


def per_device(
    out_grads, hidden_acts, routing, replica_pick, master_weights, current_slots, next_slots
):
    wide_acts = WIDE + FLAG
    input_grads, moved_weight, update = call(
        kernel,
        [((N_EP, WIDE), F32), ((WIDE, WIDE), F32), ((WIDE, WIDE), F32)],
        [
            ((WIDE, WIDE), BF16),
            ((N_Z, 32, WIDE), BF16),
            ((N_YC, N_Z, 16, 128), BF16),
            ((N_EP * 16, 128), F32),
            ((ROWS * 16, 128), F32),
            ((N_YC, N_Z, 2, 16, 128), BF16),
            ((N_Z, 2, 32, WIDE), BF16),
            ((2, WIDE, WIDE), BF16),
            ((ROWS, N_DP * WIDE), BF16),
            ((N_DP, ROWS, WIDE), BF16),
            ((N_DP, ROWS, WIDE), BF16),
            ((N_DP, ROWS, WIDE), BF16),
            ((N_DP, ROWS, WIDE), BF16),
            ((ROWS, wide_acts), BF16),
            ((ROWS, wide_acts), BF16),
            ((ROWS, wide_acts), BF16),
            ((N_DP, ROWS, wide_acts), BF16),
            ((ROWS, N_EP), BF16),
            ((N_DP, ROWS, 2 * WIDE), BF16),
            ((WIDE, WIDE), F32),
            ((WIDE, WIDE), F32),
            ((3, 128, WIDE), F32),
            ((WIDE, WIDE), F32),
            ((WIDE, WIDE), F32),
            ((CHUNKS, 3, ROWS, CHUNK), BF16),
            ((CHUNKS, 3, ROWS, CHUNK), BF16),
            ((CHUNKS, ROWS, CHUNK), F32),
            ((CHUNKS, ROWS, CHUNK), BF16),
            ((CHUNKS, ROWS, CHUNK), BF16),
            ((CHUNKS, ROWS, CHUNK), BF16),
            ((CHUNKS, ROWS, CHUNK), BF16),
        ],
        [(2,)] * 10 + [(3, 2), (2,)] + [(CHUNKS, 2)] * 3,
        0,
        out_grads,
        hidden_acts,
        routing.reshape(1, N_EP),
        replica_pick.reshape(1, N_EP),
        master_weights[0],
        current_slots.reshape(1, N_EP),
        next_slots.reshape(1, N_EP),
    )
    return (input_grads, moved_weight[None], update[None])


def solution(mesh):
    placed = (
        P(("ep", "dp"), None),
        P(("ep", "dp"), None),
        P(("ep", "dp"), None),
        P(("ep", "dp")),
        P("ep", "dp", None),
        P(),
        P(),
    )
    return jax.shard_map(
        per_device,
        mesh=mesh,
        in_specs=placed,
        out_specs=(P(("ep", "dp"), None), P("ep", "dp", None), P("ep", "dp", None)),
        check_vma=False,
    )
```

```python
import jax
import jax.numpy as jnp
from jax import lax
from jax.experimental import pallas as pl
from jax.experimental.pallas import tpu as pltpu
from jax.sharding import PartitionSpec as P

POLY_FIRST = 3.4445
POLY_SECOND = -4.775
POLY_THIRD = 2.0315
LEARNING_RATE = 0.02
UPDATE_SCALE = 0.2
EPSILON = 1e-07
PRECISE = lax.Precision.HIGHEST
BF16 = jnp.bfloat16
F32 = jnp.float32
MESH = pl.DeviceIdType.MESH
N_EP = 128
N_DP = 4
N_Z = 16
N_YC = 8
ROWS = 2 * N_EP
WIDE = 512
FLAG = 128
CHUNKS = 4
CHUNK = WIDE // CHUNKS


def span(start, size):
    return pl.ds(pl.multiple_of(start, size), size)


def wait_bytes(ref, sem):
    pltpu.make_async_copy(ref, ref, sem).wait()


def greet(z, yc, col):
    barrier = pltpu.get_barrier_semaphore()
    for k in range(1, N_Z):
        peer = lax.rem(z + k, N_Z) * N_YC + yc
        pl.semaphore_signal(barrier, inc=1, device_id={"ep": peer}, device_id_type=MESH)
    for k in range(1, N_YC):
        peer = z * N_YC + lax.rem(yc + k, N_YC)
        pl.semaphore_signal(barrier, inc=1, device_id={"ep": peer}, device_id_type=MESH)
    for k in range(1, N_DP):
        peer = lax.rem(col + k, N_DP)
        pl.semaphore_signal(barrier, inc=1, device_id={"dp": peer}, device_id_type=MESH)


def send(src, dst, sems, where):
    pltpu.make_async_remote_copy(
        src_ref=src,
        dst_ref=dst,
        send_sem=sems.at[0],
        recv_sem=sems.at[1],
        device_id=where,
        device_id_type=MESH,
    ).start()


def turn_rows(values, outer, inner):
    shape = (ROWS, ROWS)
    row = lax.broadcasted_iota(jnp.int32, shape, 0)
    column = lax.broadcasted_iota(jnp.int32, shape, 1)
    o = row // (2 * inner)
    i = lax.rem(row, 2 * inner) // 2
    p = lax.rem(row, 2)
    onehot = (column == i * (2 * outer) + o * 2 + p).astype(F32).astype(BF16)
    return jnp.dot(onehot, values, preferred_element_type=F32).astype(BF16)


def exact(left, right):
    return jnp.dot(left, right, precision=PRECISE, preferred_element_type=F32)


def pick(onehot, values):
    return jnp.dot(onehot, values, preferred_element_type=F32).astype(BF16)


def iota(shape, dimension):
    return lax.broadcasted_iota(jnp.int32, shape, dimension)


def count(mask, axis):
    return jnp.sum(mask.astype(F32), axis=axis, keepdims=True)


def plan(named, picked, now, later):
    square = (N_EP, N_EP)
    upper, lower = iota(square, 0), iota(square, 1)

    def column(row):
        return jnp.sum(jnp.where(upper == lower, row, 0.0), axis=1, keepdims=True)

    named = named.astype(F32)
    now = now.astype(F32)
    later = later.astype(F32)
    now_column = column(now)
    place = count((column(named) == named) & (upper < lower), 0)
    holders = count(now_column == named, 0)
    second = jnp.where(
        (holders == 2.0) & (lax.rem(picked, 2) == 1), 1.0, 0.0
    )
    rank_now = count((now_column == now) & (lower < upper), 1)
    rank_next = count((column(later) == later) & (upper < lower), 0)
    turned = upper == lax.rem(lower, N_Z) * N_YC + lower // N_Z
    now_turned = jnp.sum(jnp.where(turned, now_column, 0.0), axis=0, keepdims=True)
    rank_turned = jnp.sum(jnp.where(turned, rank_now, 0.0), axis=0, keepdims=True)
    tall = (ROWS, N_EP)
    row, lane = iota(tall, 0), iota(tall, 1)
    own = lane == lax.rem(row // 2, N_Z) * N_YC + row // (2 * N_Z)
    wanted = jnp.sum(jnp.where(own, later, 0.0), axis=1, keepdims=True)
    leads = jnp.sum(jnp.where(own, rank_next, 0.0), axis=1, keepdims=True) == 0.0
    pair = lax.rem(row, 2).astype(F32)
    to_slot = jnp.where((wanted == named) & (place == pair), 1.0, 0.0)
    back = jnp.where(leads, to_slot, 0.0)
    flag = jnp.sum(to_slot * second, axis=1, keepdims=True)
    hop = jnp.where((wanted == now_turned) & (rank_turned == pair), 1.0, 0.0)
    return to_slot.astype(BF16), back.astype(BF16), flag, hop.astype(BF16)


def kernel(
    og_ref, ha_ref, named_ref, pick_ref, weight_ref, now_ref, next_ref,
    out_ref, mov_ref, upd_ref,
    og_in, ha_in, weight_in, tables, home, moved, updated,
    wb, wz, wp, wide, chosen, pay, hop, w01,
    ogs, ogx, ogy, ogp, ogz, has, hy, hp, hg, back,
    lhs, grad, gram, gram_got, poly, turn,
    part_send, part_got, total, sums, bz, bp, ret,
    wz_sem, wy_sem, hopy_sem, hopz_sem, x_sem, y_sem, z_sem, hy_sem, hz_sem, hx_sem,
    g_sem, a_sem, p_sem, bz_sem, by_sem, in_sem, out_sem,
):
    me = lax.axis_index("ep")
    col = lax.axis_index("dp")
    z = me // N_YC
    yc = lax.rem(me, N_YC)

    def over_z(body):
        def step(k, carry):
            away = jnp.where(lax.rem(k, 2) == 1, (k + 1) // 2, N_Z - k // 2)
            peer = lax.rem(z + away, N_Z)
            body(peer, {"ep": peer * N_YC + yc})
            return carry

        lax.fori_loop(1, N_Z, step, 0)

    def over_yc(body):
        def step(k, carry):
            peer = lax.rem(yc + k, N_YC)
            body(peer, {"ep": z * N_YC + peer})
            return carry

        lax.fori_loop(1, N_YC, step, 0)

    my16, my32z, my32y = span(z * 16, 16), span(z * 32, 32), span(yc * 32, 32)
    my_half, my_cols = span((yc // 4) * 16, 16), span(lax.rem(yc, 4) * 128, 128)

    loads = [(weight_ref, weight_in), (og_ref, og_in), (ha_ref, ha_in)]
    loads += [(r, tables.at[i]) for i, r in enumerate((named_ref, pick_ref, now_ref, next_ref))]
    loads = [pltpu.make_async_copy(*pair, in_sem.at[i]) for i, pair in enumerate(loads)]
    for load in loads:
        load.start()
    chunks = [pl.ds(c * CHUNK, CHUNK) for c in range(CHUNKS)]
    greet(z, yc, col)

    loads[0].wait()
    wb[...] = weight_in[...].astype(BF16)
    pl.semaphore_wait(pltpu.get_barrier_semaphore(), N_Z - 1 + N_YC - 1 + N_DP - 1)
    over_z(lambda peer, there: send(wb.at[span(peer * 32, 32), :], wz.at[z], wz_sem, there))
    wz[z] = wb[my32z, :]

    for load in loads[1:]:
        load.wait()
    to_slot, leading, flag, hop_onehot = plan(*[tables[i] for i in range(4)])
    back[...] = leading
    ogs[...] = pick(to_slot, og_in[...])
    for k in range(1, N_DP):
        peer = lax.rem(col + k, N_DP)
        send(ogs.at[:, span(peer * WIDE, WIDE)], ogx.at[col], x_sem, {"dp": peer})
    has[:, :WIDE] = pick(to_slot, ha_in[...])
    has[:, WIDE:] = jnp.broadcast_to(flag, (ROWS, FLAG)).astype(BF16)
    over_yc(
        lambda peer, there: send(has.at[span(peer * 32, 32), :], hy.at[my32y, :], hy_sem, there)
    )
    hy[my32y, :] = has[my32y, :]
    ogx[col] = ogs[:, span(col * WIDE, WIDE)]

    wait_bytes(hy.at[pl.ds(0, 32 * (N_YC - 1)), :], hy_sem.at[1])
    hp[...] = turn_rows(hy[...], N_Z, N_YC)
    over_z(
        lambda peer, there: send(
            hp.at[span(peer * 16, 16), :], hg.at[col, my16, :], hz_sem, there
        )
    )
    hg[col, my16, :] = hp[my16, :]

    wait_bytes(ogx.at[pl.ds(0, N_DP - 1)], x_sem.at[1])
    over_yc(
        lambda peer, there: send(
            ogx.at[:, span(peer * 32, 32), :], ogy.at[:, my32y, :], y_sem, there
        )
    )
    ogy[:, my32y, :] = ogx[:, my32y, :]

    wait_bytes(wz.at[pl.ds(0, N_Z - 1)], wz_sem.at[1])
    over_yc(
        lambda peer, there: send(
            wz.at[:, span((peer // 4) * 16, 16), span(lax.rem(peer, 4) * 128, 128)],
            wp.at[yc], wy_sem, there,
        )
    )
    wp[yc] = wz[:, my_half, my_cols]

    wait_bytes(ogy.at[:, pl.ds(0, 32 * (N_YC - 1)), :], y_sem.at[1])
    for g in range(N_DP):
        ogp[g] = turn_rows(ogy[g], N_Z, N_YC)
    over_z(
        lambda peer, there: send(
            ogp.at[:, span(peer * 16, 16), :], ogz.at[:, my16, :], z_sem, there
        )
    )
    ogz[:, my16, :] = ogp[:, my16, :]

    wait_bytes(wp.at[pl.ds(0, N_YC - 1)], wy_sem.at[1])
    wide[...] = wp[...].reshape(N_EP * 16, 128).astype(F32)
    for j in range(16):
        piece = wide[pl.ds(j, N_EP, stride=16), :].astype(BF16)
        chosen[pl.ds(j, ROWS, stride=16), :] = jnp.dot(
            hop_onehot, piece, preferred_element_type=F32
        )
    pay[...] = chosen[...].astype(BF16).reshape(N_YC, N_Z, 2, 16, 128)
    over_yc(
        lambda peer, there: send(
            pay.at[peer], hop.at[:, :, my_half, my_cols], hopy_sem, there
        )
    )
    hop[:, :, my_half, my_cols] = pay[yc]

    wait_bytes(hp.at[pl.ds(0, 16 * (N_Z - 1)), :], hz_sem.at[1])
    for k in range(1, N_DP):
        peer = lax.rem(col + k, N_DP)
        send(hg.at[col], hg.at[col], hx_sem, {"dp": peer})

    wait_bytes(pay.at[pl.ds(0, N_YC - 1)], hopy_sem.at[1])
    for lanes, sem in zip(chunks, range(CHUNKS)):
        over_z(
            lambda peer, there: send(
                hop.at[peer, :, :, lanes], w01.at[:, my32z, lanes], hopz_sem.at[sem], there
            )
        )
    w01[:, my32z, :] = hop[z]

    def partials(c):
        wait_bytes(hop.at[pl.ds(0, N_Z - 1), :, :, chunks[c]], hopz_sem.at[c, 1])
        weight = w01[:, :, chunks[c]].reshape(2 * WIDE, CHUNK)
        for k in (1, 2, 3, 0):
            g = lax.rem(col + k, N_DP)
            product = jnp.dot(lhs[g], weight, preferred_element_type=F32)
            if k:
                part_send[c, k - 1] = product.astype(BF16)
                send(part_send.at[c, k - 1], part_got.at[c, k - 1], p_sem.at[c], {"dp": g})
            else:
                total[c] = product

    def add_up(c):
        wait_bytes(part_got.at[c], p_sem.at[c, 1])
        got = part_got[c].astype(F32)
        sums[c] = (total[c] + got[0] + got[1] + got[2]).astype(BF16)

    def home_z(c):
        over_z(
            lambda peer, there: send(
                sums.at[c, span(peer * 16, 16), :], bz.at[c, my16, :], bz_sem.at[c], there
            )
        )
        bz[c, my16, :] = sums[c, my16, :]

    def home_yc(c):
        wait_bytes(bz.at[c, pl.ds(0, 16 * (N_Z - 1)), :], bz_sem.at[c, 1])
        bp[c] = turn_rows(bz[c], N_YC, N_Z)
        over_yc(
            lambda peer, there: send(
                bp.at[c, span(peer * 32, 32), :], ret.at[c, my32y, :], by_sem.at[c], there
            )
        )
        ret[c, my32y, :] = bp[c, my32y, :]

    wait_bytes(hg.at[pl.ds(0, N_DP - 1)], hx_sem.at[1])
    wait_bytes(ogz.at[:, pl.ds(0, 16 * (N_Z - 1)), :], z_sem.at[1])
    acts = hg[:, :, :WIDE].reshape(N_DP * ROWS, WIDE)
    for c in range(0, WIDE, 256):
        grad[c : c + 256, :] = lax.dot_general(
            ogz[:, :, c : c + 256].reshape(N_DP * ROWS, 256),
            acts,
            (((0,), (0,)), ((), ())),
            preferred_element_type=F32,
        )

    for k in (1, 2, 3, 0):
        peer = lax.rem(col + k, N_DP)
        block = span(peer * 128, 128)
        gram[block, :] = exact(grad[:, block].T, grad[...])
        if k:
            send(gram.at[block, :], gram_got.at[k - 1], g_sem.at[k - 1], {"dp": peer})
    for g in range(N_DP):
        second = jnp.concatenate([hg[g, :, WIDE:]] * (WIDE // FLAG), axis=1).astype(F32)
        rows = ogz[g].astype(F32)
        lhs[g, :, :WIDE] = (rows * (1.0 - second)).astype(BF16)
        lhs[g, :, WIDE:] = (rows * second).astype(BF16)
    share = gram[span(col * 128, 128), :]
    for k in range(1, N_DP):
        wait_bytes(gram_got.at[k - 1], g_sem.at[k - 1, 1])
        share = share + gram_got[k - 1]
    poly[span(col * 128, 128), :] = share
    for k in range(1, N_DP):
        peer = lax.rem(col + k, N_DP)
        send(
            poly.at[span(col * 128, 128), :], poly.at[span(col * 128, 128), :], a_sem,
            {"dp": peer},
        )
    for k in range(1, N_DP):
        wait_bytes(gram_got.at[k - 1], g_sem.at[k - 1, 0])
    wait_bytes(gram_got, a_sem.at[1])
    wait_bytes(gram_got, a_sem.at[0])

    eye = jnp.where(iota((WIDE, WIDE), 0) == iota((WIDE, WIDE), 1), 1.0, 0.0)
    square = jnp.sum(poly[...] * eye, keepdims=True)
    scale = 1.0 / (jnp.sqrt(square) + EPSILON)
    a1 = poly[...] * scale * scale
    q1 = POLY_FIRST * eye + POLY_SECOND * a1 + POLY_THIRD * exact(a1, a1)
    a2 = exact(exact(q1, a1), q1)
    partials(0)
    q2 = POLY_FIRST * eye + POLY_SECOND * a2 + POLY_THIRD * exact(a2, a2)
    turn[...] = exact(q1, q2) * (scale * (UPDATE_SCALE * (N_DP * WIDE) ** 0.5))
    partials(1)
    add_up(0)
    updated[...] = exact(grad[...], turn[...])
    save_update = pltpu.make_async_copy(updated, upd_ref, out_sem.at[0])
    save_update.start()

    partials(2)
    add_up(1)
    partials(3)
    for c in range(2):
        home_z(c)
    add_up(2)
    home_z(2)
    moved[...] = w01[0].astype(F32) - LEARNING_RATE * updated[...]
    save_moved = pltpu.make_async_copy(moved, mov_ref, out_sem.at[1])
    save_moved.start()
    add_up(3)
    home_z(3)
    for c in range(CHUNKS):
        home_yc(c)
    for c in range(CHUNKS):
        wait_bytes(ret.at[c, pl.ds(0, 32 * (N_YC - 1)), :], by_sem.at[c, 1])
        home[:, chunks[c]] = lax.dot_general(
            back[...], ret[c], (((0,), (0,)), ((), ())), preferred_element_type=F32
        )
    save_home = pltpu.make_async_copy(home, out_ref, out_sem.at[2])
    save_home.start()

    for c in range(CHUNKS):
        wait_bytes(part_got.at[c], p_sem.at[c, 0])
        wait_bytes(bz.at[c, pl.ds(0, 16 * (N_Z - 1)), :], bz_sem.at[c, 0])
        wait_bytes(ret.at[c, pl.ds(0, 32 * (N_YC - 1)), :], by_sem.at[c, 0])
    wait_bytes(wz.at[pl.ds(0, N_Z - 1)], wz_sem.at[0])
    wait_bytes(wp.at[pl.ds(0, N_YC - 1)], wy_sem.at[0])
    wait_bytes(pay.at[pl.ds(0, N_YC - 1)], hopy_sem.at[0])
    for c in range(CHUNKS):
        wait_bytes(hop.at[pl.ds(0, N_Z - 1), :, :, chunks[c]], hopz_sem.at[c, 0])
    wait_bytes(ogx.at[pl.ds(0, N_DP - 1)], x_sem.at[0])
    wait_bytes(ogy.at[:, pl.ds(0, 32 * (N_YC - 1)), :], y_sem.at[0])
    wait_bytes(ogz.at[:, pl.ds(0, 16 * (N_Z - 1)), :], z_sem.at[0])
    wait_bytes(hy.at[pl.ds(0, 32 * (N_YC - 1)), :], hy_sem.at[0])
    wait_bytes(hp.at[pl.ds(0, 16 * (N_Z - 1)), :], hz_sem.at[0])
    wait_bytes(hg.at[pl.ds(0, N_DP - 1)], hx_sem.at[0])
    save_update.wait()
    save_moved.wait()
    save_home.wait()


def call(kernel, outs, scratch, semaphores, collective_id, *args):
    hbm = pl.BlockSpec(memory_space=pltpu.HBM)
    return pl.pallas_call(
        kernel,
        out_shape=[jax.ShapeDtypeStruct(*o) for o in outs],
        in_specs=[hbm] * len(args),
        out_specs=[hbm] * len(outs),
        scratch_shapes=[pltpu.VMEM(*s) for s in scratch]
        + [pltpu.SemaphoreType.DMA(s) for s in semaphores],
        compiler_params=pltpu.CompilerParams(
            collective_id=collective_id, has_side_effects=True, vmem_limit_bytes=58 * 2**20
        ),
    )(*args)


def per_device(
    out_grads, hidden_acts, routing, replica_pick, master_weights, current_slots, next_slots
):
    wide_acts = WIDE + FLAG
    input_grads, moved_weight, update = call(
        kernel,
        [((N_EP, WIDE), F32), ((WIDE, WIDE), F32), ((WIDE, WIDE), F32)],
        [
            ((N_EP, N_DP * WIDE), BF16),
            ((N_EP, WIDE), BF16),
            ((WIDE, WIDE), F32),
            ((4, 1, N_EP), jnp.int32),
            ((N_EP, WIDE), F32),
            ((WIDE, WIDE), F32),
            ((WIDE, WIDE), F32),
            ((WIDE, WIDE), BF16),
            ((N_Z, 32, WIDE), BF16),
            ((N_YC, N_Z, 16, 128), BF16),
            ((N_EP * 16, 128), F32),
            ((ROWS * 16, 128), F32),
            ((N_YC, N_Z, 2, 16, 128), BF16),
            ((N_Z, 2, 32, WIDE), BF16),
            ((2, WIDE, WIDE), BF16),
            ((ROWS, N_DP * WIDE), BF16),
            ((N_DP, ROWS, WIDE), BF16),
            ((N_DP, ROWS, WIDE), BF16),
            ((N_DP, ROWS, WIDE), BF16),
            ((N_DP, ROWS, WIDE), BF16),
            ((ROWS, wide_acts), BF16),
            ((ROWS, wide_acts), BF16),
            ((ROWS, wide_acts), BF16),
            ((N_DP, ROWS, wide_acts), BF16),
            ((ROWS, N_EP), BF16),
            ((N_DP, ROWS, 2 * WIDE), BF16),
            ((WIDE, WIDE), F32),
            ((WIDE, WIDE), F32),
            ((3, 128, WIDE), F32),
            ((WIDE, WIDE), F32),
            ((WIDE, WIDE), F32),
            ((CHUNKS, 3, ROWS, CHUNK), BF16),
            ((CHUNKS, 3, ROWS, CHUNK), BF16),
            ((CHUNKS, ROWS, CHUNK), F32),
            ((CHUNKS, ROWS, CHUNK), BF16),
            ((CHUNKS, ROWS, CHUNK), BF16),
            ((CHUNKS, ROWS, CHUNK), BF16),
            ((CHUNKS, ROWS, CHUNK), BF16),
        ],
        [(2,)] * 3 + [(CHUNKS, 2)] + [(2,)] * 6 + [(3, 2), (2,)] + [(CHUNKS, 2)] * 3 + [(7,), (3,)],
        0,
        out_grads,
        hidden_acts,
        routing.reshape(1, N_EP),
        replica_pick.reshape(1, N_EP),
        master_weights[0],
        current_slots.reshape(1, N_EP),
        next_slots.reshape(1, N_EP),
    )
    return (input_grads, moved_weight[None], update[None])


def solution(mesh):
    placed = (
        P(("ep", "dp"), None),
        P(("ep", "dp"), None),
        P(("ep", "dp"), None),
        P(("ep", "dp")),
        P("ep", "dp", None),
        P(),
        P(),
    )
    return jax.shard_map(
        per_device,
        mesh=mesh,
        in_specs=placed,
        out_specs=(P(("ep", "dp"), None), P("ep", "dp", None), P("ep", "dp", None)),
        check_vma=False,
    )
```

```python
import jax
import jax.numpy as jnp
from jax import lax
from jax.experimental import pallas as pl
from jax.experimental.pallas import tpu as pltpu
from jax.sharding import PartitionSpec as P

POLY_FIRST = 3.4445
POLY_SECOND = -4.775
POLY_THIRD = 2.0315
LEARNING_RATE = 0.02
UPDATE_SCALE = 0.2
EPSILON = 1e-07
PRECISE = lax.Precision.HIGHEST
BF16 = jnp.bfloat16
F32 = jnp.float32
MESH = pl.DeviceIdType.MESH
N_EP = 128
N_DP = 4
N_Z = 16
N_YC = 8
ROWS = 2 * N_EP
WIDE = 512
FLAG = 128
CHUNKS = 4
CHUNK = WIDE // CHUNKS


def span(start, size):
    return pl.ds(pl.multiple_of(start, size), size)


def wait_bytes(ref, sem):
    pltpu.make_async_copy(ref, ref, sem).wait()


def greet(z, yc, col):
    barrier = pltpu.get_barrier_semaphore()
    for k in range(1, N_Z):
        peer = lax.rem(z + k, N_Z) * N_YC + yc
        pl.semaphore_signal(barrier, inc=1, device_id={"ep": peer}, device_id_type=MESH)
    for k in range(1, N_YC):
        peer = z * N_YC + lax.rem(yc + k, N_YC)
        pl.semaphore_signal(barrier, inc=1, device_id={"ep": peer}, device_id_type=MESH)
    for k in range(1, N_DP):
        peer = lax.rem(col + k, N_DP)
        pl.semaphore_signal(barrier, inc=1, device_id={"dp": peer}, device_id_type=MESH)


def send(src, dst, sems, where):
    pltpu.make_async_remote_copy(
        src_ref=src,
        dst_ref=dst,
        send_sem=sems.at[0],
        recv_sem=sems.at[1],
        device_id=where,
        device_id_type=MESH,
    ).start()


def turn_rows(values, outer, inner):
    shape = (ROWS, ROWS)
    row = lax.broadcasted_iota(jnp.int32, shape, 0)
    column = lax.broadcasted_iota(jnp.int32, shape, 1)
    o = row // (2 * inner)
    i = lax.rem(row, 2 * inner) // 2
    p = lax.rem(row, 2)
    onehot = (column == i * (2 * outer) + o * 2 + p).astype(F32).astype(BF16)
    return jnp.dot(onehot, values, preferred_element_type=F32).astype(BF16)


def exact(left, right):
    return jnp.dot(left, right, precision=PRECISE, preferred_element_type=F32)


def pick(onehot, values):
    return jnp.dot(onehot, values, preferred_element_type=F32).astype(BF16)


def iota(shape, dimension):
    return lax.broadcasted_iota(jnp.int32, shape, dimension)


def count(mask, axis):
    return jnp.sum(mask.astype(F32), axis=axis, keepdims=True)


def plan(named, picked, now, later):
    square = (N_EP, N_EP)
    upper, lower = iota(square, 0), iota(square, 1)

    def column(row):
        return jnp.sum(jnp.where(upper == lower, row, 0.0), axis=1, keepdims=True)

    named = named.astype(F32)
    now = now.astype(F32)
    later = later.astype(F32)
    now_column = column(now)
    place = count((column(named) == named) & (upper < lower), 0)
    holders = count(now_column == named, 0)
    second = jnp.where(
        (holders == 2.0) & (lax.rem(picked, 2) == 1), 1.0, 0.0
    )
    rank_now = count((now_column == now) & (lower < upper), 1)
    rank_next = count((column(later) == later) & (upper < lower), 0)
    turned = upper == lax.rem(lower, N_Z) * N_YC + lower // N_Z
    now_turned = jnp.sum(jnp.where(turned, now_column, 0.0), axis=0, keepdims=True)
    rank_turned = jnp.sum(jnp.where(turned, rank_now, 0.0), axis=0, keepdims=True)
    tall = (ROWS, N_EP)
    row, lane = iota(tall, 0), iota(tall, 1)
    own = lane == lax.rem(row // 2, N_Z) * N_YC + row // (2 * N_Z)
    wanted = jnp.sum(jnp.where(own, later, 0.0), axis=1, keepdims=True)
    leads = jnp.sum(jnp.where(own, rank_next, 0.0), axis=1, keepdims=True) == 0.0
    pair = lax.rem(row, 2).astype(F32)
    to_slot = jnp.where((wanted == named) & (place == pair), 1.0, 0.0)
    back = jnp.where(leads, to_slot, 0.0)
    flag = jnp.sum(to_slot * second, axis=1, keepdims=True)
    hop = jnp.where((wanted == now_turned) & (rank_turned == pair), 1.0, 0.0)
    return to_slot.astype(BF16), back.astype(BF16), flag, hop.astype(BF16)


def kernel(
    og_ref, ha_ref, named_ref, pick_ref, weight_ref, now_ref, next_ref,
    ret, back, w01, upd_ref,
    og_in, ha_in, weight_in, tables, updated,
    wb, wz, wp, wide, chosen, pay, hop,
    ogs, ogx, ogy, ogp, ogz, has, hy, hp, hg,
    lhs, grad, gram, gram_got, poly, turn,
    part_send, part_got, total, sums, bz, bp,
    wz_sem, wy_sem, hopy_sem, hopz_sem, x_sem, y_sem, z_sem, hy_sem, hz_sem, hx_sem,
    g_sem, a_sem, p_sem, bz_sem, by_sem, in_sem, out_sem,
):
    me = lax.axis_index("ep")
    col = lax.axis_index("dp")
    z = me // N_YC
    yc = lax.rem(me, N_YC)

    def over_z(body):
        def step(k, carry):
            away = jnp.where(lax.rem(k, 2) == 1, (k + 1) // 2, N_Z - k // 2)
            peer = lax.rem(z + away, N_Z)
            body(peer, {"ep": peer * N_YC + yc})
            return carry

        lax.fori_loop(1, N_Z, step, 0)

    def over_yc(body):
        def step(k, carry):
            peer = lax.rem(yc + k, N_YC)
            body(peer, {"ep": z * N_YC + peer})
            return carry

        lax.fori_loop(1, N_YC, step, 0)

    my16, my32z, my32y = span(z * 16, 16), span(z * 32, 32), span(yc * 32, 32)
    my_half, my_cols = span((yc // 4) * 16, 16), span(lax.rem(yc, 4) * 128, 128)

    loads = [(weight_ref, weight_in), (og_ref, og_in), (ha_ref, ha_in)]
    loads += [(r, tables.at[i]) for i, r in enumerate((named_ref, pick_ref, now_ref, next_ref))]
    loads = [pltpu.make_async_copy(*pair, in_sem.at[i]) for i, pair in enumerate(loads)]
    for load in loads:
        load.start()
    chunks = [pl.ds(c * CHUNK, CHUNK) for c in range(CHUNKS)]
    greet(z, yc, col)

    loads[0].wait()
    wb[...] = weight_in[...].astype(BF16)
    pl.semaphore_wait(pltpu.get_barrier_semaphore(), N_Z - 1 + N_YC - 1 + N_DP - 1)
    over_z(lambda peer, there: send(wb.at[span(peer * 32, 32), :], wz.at[z], wz_sem, there))
    wz[z] = wb[my32z, :]

    for load in loads[1:]:
        load.wait()
    to_slot, leading, flag, hop_onehot = plan(*[tables[i] for i in range(4)])
    back[...] = leading
    ogs[...] = pick(to_slot, og_in[...])
    for k in range(1, N_DP):
        peer = lax.rem(col + k, N_DP)
        send(ogs.at[:, span(peer * WIDE, WIDE)], ogx.at[col], x_sem, {"dp": peer})
    has[:, :WIDE] = pick(to_slot, ha_in[...])
    has[:, WIDE:] = jnp.broadcast_to(flag, (ROWS, FLAG)).astype(BF16)
    over_yc(
        lambda peer, there: send(has.at[span(peer * 32, 32), :], hy.at[my32y, :], hy_sem, there)
    )
    hy[my32y, :] = has[my32y, :]
    ogx[col] = ogs[:, span(col * WIDE, WIDE)]

    wait_bytes(hy.at[pl.ds(0, 32 * (N_YC - 1)), :], hy_sem.at[1])
    hp[...] = turn_rows(hy[...], N_Z, N_YC)
    over_z(
        lambda peer, there: send(
            hp.at[span(peer * 16, 16), :], hg.at[col, my16, :], hz_sem, there
        )
    )
    hg[col, my16, :] = hp[my16, :]

    wait_bytes(ogx.at[pl.ds(0, N_DP - 1)], x_sem.at[1])
    over_yc(
        lambda peer, there: send(
            ogx.at[:, span(peer * 32, 32), :], ogy.at[:, my32y, :], y_sem, there
        )
    )
    ogy[:, my32y, :] = ogx[:, my32y, :]

    wait_bytes(wz.at[pl.ds(0, N_Z - 1)], wz_sem.at[1])
    over_yc(
        lambda peer, there: send(
            wz.at[:, span((peer // 4) * 16, 16), span(lax.rem(peer, 4) * 128, 128)],
            wp.at[yc], wy_sem, there,
        )
    )
    wp[yc] = wz[:, my_half, my_cols]

    wait_bytes(ogy.at[:, pl.ds(0, 32 * (N_YC - 1)), :], y_sem.at[1])
    for g in range(N_DP):
        ogp[g] = turn_rows(ogy[g], N_Z, N_YC)
    over_z(
        lambda peer, there: send(
            ogp.at[:, span(peer * 16, 16), :], ogz.at[:, my16, :], z_sem, there
        )
    )
    ogz[:, my16, :] = ogp[:, my16, :]

    wait_bytes(wp.at[pl.ds(0, N_YC - 1)], wy_sem.at[1])
    wide[...] = wp[...].reshape(N_EP * 16, 128).astype(F32)
    for j in range(16):
        piece = wide[pl.ds(j, N_EP, stride=16), :].astype(BF16)
        chosen[pl.ds(j, ROWS, stride=16), :] = jnp.dot(
            hop_onehot, piece, preferred_element_type=F32
        )
    pay[...] = chosen[...].astype(BF16).reshape(N_YC, N_Z, 2, 16, 128)
    over_yc(
        lambda peer, there: send(
            pay.at[peer], hop.at[:, :, my_half, my_cols], hopy_sem, there
        )
    )
    hop[:, :, my_half, my_cols] = pay[yc]

    wait_bytes(hp.at[pl.ds(0, 16 * (N_Z - 1)), :], hz_sem.at[1])
    for k in range(1, N_DP):
        peer = lax.rem(col + k, N_DP)
        send(hg.at[col], hg.at[col], hx_sem, {"dp": peer})

    wait_bytes(pay.at[pl.ds(0, N_YC - 1)], hopy_sem.at[1])
    for lanes, sem in zip(chunks, range(CHUNKS)):
        over_z(
            lambda peer, there: send(
                hop.at[peer, :, :, lanes], w01.at[:, my32z, lanes], hopz_sem.at[sem], there
            )
        )
    w01[:, my32z, :] = hop[z]

    def partials(c):
        wait_bytes(hop.at[pl.ds(0, N_Z - 1), :, :, chunks[c]], hopz_sem.at[c, 1])
        weight = w01[:, :, chunks[c]].reshape(2 * WIDE, CHUNK)
        for k in (1, 2, 3, 0):
            g = lax.rem(col + k, N_DP)
            product = jnp.dot(lhs[g], weight, preferred_element_type=F32)
            if k:
                part_send[c, k - 1] = product.astype(BF16)
                send(part_send.at[c, k - 1], part_got.at[c, k - 1], p_sem.at[c], {"dp": g})
            else:
                total[c] = product

    def add_up(c):
        wait_bytes(part_got.at[c], p_sem.at[c, 1])
        got = part_got[c].astype(F32)
        sums[c] = (total[c] + got[0] + got[1] + got[2]).astype(BF16)

    def home_z(c):
        over_z(
            lambda peer, there: send(
                sums.at[c, span(peer * 16, 16), :], bz.at[c, my16, :], bz_sem.at[c], there
            )
        )
        bz[c, my16, :] = sums[c, my16, :]

    def home_yc(c):
        wait_bytes(bz.at[c, pl.ds(0, 16 * (N_Z - 1)), :], bz_sem.at[c, 1])
        bp[c] = turn_rows(bz[c], N_YC, N_Z)
        over_yc(
            lambda peer, there: send(
                bp.at[c, span(peer * 32, 32), :], ret.at[my32y, chunks[c]], by_sem.at[c], there
            )
        )
        ret[my32y, chunks[c]] = bp[c, my32y, :]

    wait_bytes(hg.at[pl.ds(0, N_DP - 1)], hx_sem.at[1])
    wait_bytes(ogz.at[:, pl.ds(0, 16 * (N_Z - 1)), :], z_sem.at[1])
    acts = hg[:, :, :WIDE].reshape(N_DP * ROWS, WIDE)
    for c in range(0, WIDE, 256):
        grad[c : c + 256, :] = lax.dot_general(
            ogz[:, :, c : c + 256].reshape(N_DP * ROWS, 256),
            acts,
            (((0,), (0,)), ((), ())),
            preferred_element_type=F32,
        )

    for k in (1, 2, 3, 0):
        peer = lax.rem(col + k, N_DP)
        block = span(peer * 128, 128)
        gram[block, :] = exact(grad[:, block].T, grad[...])
        if k:
            send(gram.at[block, :], gram_got.at[k - 1], g_sem.at[k - 1], {"dp": peer})
    for g in range(N_DP):
        second = jnp.concatenate([hg[g, :, WIDE:]] * (WIDE // FLAG), axis=1).astype(F32)
        rows = ogz[g].astype(F32)
        lhs[g, :, :WIDE] = (rows * (1.0 - second)).astype(BF16)
        lhs[g, :, WIDE:] = (rows * second).astype(BF16)
    share = gram[span(col * 128, 128), :]
    for k in range(1, N_DP):
        wait_bytes(gram_got.at[k - 1], g_sem.at[k - 1, 1])
        share = share + gram_got[k - 1]
    poly[span(col * 128, 128), :] = share
    for k in range(1, N_DP):
        peer = lax.rem(col + k, N_DP)
        send(
            poly.at[span(col * 128, 128), :], poly.at[span(col * 128, 128), :], a_sem,
            {"dp": peer},
        )
    for k in range(1, N_DP):
        wait_bytes(gram_got.at[k - 1], g_sem.at[k - 1, 0])
    wait_bytes(gram_got, a_sem.at[1])
    wait_bytes(gram_got, a_sem.at[0])

    eye = jnp.where(iota((WIDE, WIDE), 0) == iota((WIDE, WIDE), 1), 1.0, 0.0)
    square = jnp.sum(poly[...] * eye, keepdims=True)
    scale = 1.0 / (jnp.sqrt(square) + EPSILON)
    a1 = poly[...] * scale * scale
    q1 = POLY_FIRST * eye + POLY_SECOND * a1 + POLY_THIRD * exact(a1, a1)
    a2 = exact(exact(q1, a1), q1)
    partials(0)
    q2 = POLY_FIRST * eye + POLY_SECOND * a2 + POLY_THIRD * exact(a2, a2)
    turn[...] = exact(q1, q2) * (scale * (UPDATE_SCALE * (N_DP * WIDE) ** 0.5))
    partials(1)
    add_up(0)
    updated[...] = exact(grad[...], turn[...])
    save_update = pltpu.make_async_copy(updated, upd_ref, out_sem)
    save_update.start()

    partials(2)
    add_up(1)
    partials(3)
    for c in range(2):
        home_z(c)
    add_up(2)
    home_z(2)
    add_up(3)
    home_z(3)
    for c in range(CHUNKS):
        home_yc(c)
    for c in range(CHUNKS):
        wait_bytes(ret.at[pl.ds(0, 32 * (N_YC - 1)), chunks[c]], by_sem.at[c, 1])

    for c in range(CHUNKS):
        wait_bytes(part_got.at[c], p_sem.at[c, 0])
        wait_bytes(bz.at[c, pl.ds(0, 16 * (N_Z - 1)), :], bz_sem.at[c, 0])
        wait_bytes(ret.at[pl.ds(0, 32 * (N_YC - 1)), chunks[c]], by_sem.at[c, 0])
    wait_bytes(wz.at[pl.ds(0, N_Z - 1)], wz_sem.at[0])
    wait_bytes(wp.at[pl.ds(0, N_YC - 1)], wy_sem.at[0])
    wait_bytes(pay.at[pl.ds(0, N_YC - 1)], hopy_sem.at[0])
    for c in range(CHUNKS):
        wait_bytes(hop.at[pl.ds(0, N_Z - 1), :, :, chunks[c]], hopz_sem.at[c, 0])
    wait_bytes(ogx.at[pl.ds(0, N_DP - 1)], x_sem.at[0])
    wait_bytes(ogy.at[:, pl.ds(0, 32 * (N_YC - 1)), :], y_sem.at[0])
    wait_bytes(ogz.at[:, pl.ds(0, 16 * (N_Z - 1)), :], z_sem.at[0])
    wait_bytes(hy.at[pl.ds(0, 32 * (N_YC - 1)), :], hy_sem.at[0])
    wait_bytes(hp.at[pl.ds(0, 16 * (N_Z - 1)), :], hz_sem.at[0])
    wait_bytes(hg.at[pl.ds(0, N_DP - 1)], hx_sem.at[0])
    save_update.wait()


def call(kernel, outs, scratch, semaphores, collective_id, *args):
    vmem = pl.BlockSpec(memory_space=pltpu.VMEM)
    hbm = pl.BlockSpec(memory_space=pltpu.HBM)
    return pl.pallas_call(
        kernel,
        out_shape=[jax.ShapeDtypeStruct(*o) for o in outs],
        in_specs=[hbm] * len(args),
        out_specs=[vmem] * (len(outs) - 1) + [hbm],
        scratch_shapes=[pltpu.VMEM(*s) for s in scratch]
        + [pltpu.SemaphoreType.DMA(s) for s in semaphores],
        compiler_params=pltpu.CompilerParams(
            collective_id=collective_id, has_side_effects=True, vmem_limit_bytes=58 * 2**20
        ),
    )(*args)


def per_device(
    out_grads, hidden_acts, routing, replica_pick, master_weights, current_slots, next_slots
):
    wide_acts = WIDE + FLAG
    returned, back, moved, update = call(
        kernel,
        [
            ((ROWS, WIDE), BF16),
            ((ROWS, N_EP), BF16),
            ((2, WIDE, WIDE), BF16),
            ((WIDE, WIDE), F32),
        ],
        [
            ((N_EP, N_DP * WIDE), BF16),
            ((N_EP, WIDE), BF16),
            ((WIDE, WIDE), F32),
            ((4, 1, N_EP), jnp.int32),
            ((WIDE, WIDE), F32),
            ((WIDE, WIDE), BF16),
            ((N_Z, 32, WIDE), BF16),
            ((N_YC, N_Z, 16, 128), BF16),
            ((N_EP * 16, 128), F32),
            ((ROWS * 16, 128), F32),
            ((N_YC, N_Z, 2, 16, 128), BF16),
            ((N_Z, 2, 32, WIDE), BF16),
            ((ROWS, N_DP * WIDE), BF16),
            ((N_DP, ROWS, WIDE), BF16),
            ((N_DP, ROWS, WIDE), BF16),
            ((N_DP, ROWS, WIDE), BF16),
            ((N_DP, ROWS, WIDE), BF16),
            ((ROWS, wide_acts), BF16),
            ((ROWS, wide_acts), BF16),
            ((ROWS, wide_acts), BF16),
            ((N_DP, ROWS, wide_acts), BF16),
            ((N_DP, ROWS, 2 * WIDE), BF16),
            ((WIDE, WIDE), F32),
            ((WIDE, WIDE), F32),
            ((3, 128, WIDE), F32),
            ((WIDE, WIDE), F32),
            ((WIDE, WIDE), F32),
            ((CHUNKS, 3, ROWS, CHUNK), BF16),
            ((CHUNKS, 3, ROWS, CHUNK), BF16),
            ((CHUNKS, ROWS, CHUNK), F32),
            ((CHUNKS, ROWS, CHUNK), BF16),
            ((CHUNKS, ROWS, CHUNK), BF16),
            ((CHUNKS, ROWS, CHUNK), BF16),
        ],
        [(2,)] * 3 + [(CHUNKS, 2)] + [(2,)] * 6 + [(3, 2), (2,)] + [(CHUNKS, 2)] * 3 + [(7,), ()],
        0,
        out_grads,
        hidden_acts,
        routing.reshape(1, N_EP),
        replica_pick.reshape(1, N_EP),
        master_weights[0],
        current_slots.reshape(1, N_EP),
        next_slots.reshape(1, N_EP),
    )
    input_grads = lax.dot_general(
        back, returned, (((0,), (0,)), ((), ())), preferred_element_type=F32
    )
    moved_weight = moved[0].astype(F32) - LEARNING_RATE * update
    return (input_grads, moved_weight[None], update[None])


def solution(mesh):
    placed = (
        P(("ep", "dp"), None),
        P(("ep", "dp"), None),
        P(("ep", "dp"), None),
        P(("ep", "dp")),
        P("ep", "dp", None),
        P(),
        P(),
    )
    return jax.shard_map(
        per_device,
        mesh=mesh,
        in_specs=placed,
        out_specs=(P(("ep", "dp"), None), P("ep", "dp", None), P("ep", "dp", None)),
        check_vma=False,
    )
```

```python
import jax
import jax.numpy as jnp
from jax import lax
from jax.experimental import pallas as pl
from jax.experimental.pallas import tpu as pltpu
from jax.sharding import PartitionSpec as P

POLY_FIRST = 3.4445
POLY_SECOND = -4.775
POLY_THIRD = 2.0315
LEARNING_RATE = 0.02
UPDATE_SCALE = 0.2
EPSILON = 1e-07
PRECISE = lax.Precision.HIGHEST
BF16 = jnp.bfloat16
F32 = jnp.float32
MESH = pl.DeviceIdType.MESH
N_EP = 128
N_DP = 4
N_Z = 16
N_YC = 8
ROWS = 2 * N_EP
WIDE = 512
FLAG = 128
CHUNKS = 2
CHUNK = WIDE // CHUNKS


def span(start, size):
    return pl.ds(pl.multiple_of(start, size), size)


def wait_bytes(ref, sem):
    pltpu.make_async_copy(ref, ref, sem).wait()


def greet(z, yc, col):
    barrier = pltpu.get_barrier_semaphore()
    for k in range(1, N_Z):
        peer = lax.rem(z + k, N_Z) * N_YC + yc
        pl.semaphore_signal(barrier, inc=1, device_id={"ep": peer}, device_id_type=MESH)
    for k in range(1, N_YC):
        peer = z * N_YC + lax.rem(yc + k, N_YC)
        pl.semaphore_signal(barrier, inc=1, device_id={"ep": peer}, device_id_type=MESH)
    for k in range(1, N_DP):
        peer = lax.rem(col + k, N_DP)
        pl.semaphore_signal(barrier, inc=1, device_id={"dp": peer}, device_id_type=MESH)


def send(src, dst, sems, where):
    pltpu.make_async_remote_copy(
        src_ref=src,
        dst_ref=dst,
        send_sem=sems.at[0],
        recv_sem=sems.at[1],
        device_id=where,
        device_id_type=MESH,
    ).start()


def turn_rows(values, outer, inner):
    shape = (ROWS, ROWS)
    row = lax.broadcasted_iota(jnp.int32, shape, 0)
    column = lax.broadcasted_iota(jnp.int32, shape, 1)
    o = row // (2 * inner)
    i = lax.rem(row, 2 * inner) // 2
    p = lax.rem(row, 2)
    onehot = (column == i * (2 * outer) + o * 2 + p).astype(F32).astype(BF16)
    return jnp.dot(onehot, values, preferred_element_type=F32).astype(BF16)


def exact(left, right):
    return jnp.dot(left, right, precision=PRECISE, preferred_element_type=F32)


def pick(onehot, values):
    return jnp.dot(onehot, values, preferred_element_type=F32).astype(BF16)


def iota(shape, dimension):
    return lax.broadcasted_iota(jnp.int32, shape, dimension)


def count(mask, axis):
    return jnp.sum(mask.astype(F32), axis=axis, keepdims=True)


def plan(named, picked, now, later):
    square = (N_EP, N_EP)
    upper, lower = iota(square, 0), iota(square, 1)

    def column(row):
        return jnp.sum(jnp.where(upper == lower, row, 0.0), axis=1, keepdims=True)

    named = named.astype(F32)
    now = now.astype(F32)
    later = later.astype(F32)
    now_column = column(now)
    place = count((column(named) == named) & (upper < lower), 0)
    holders = count(now_column == named, 0)
    second = jnp.where(
        (holders == 2.0) & (lax.rem(picked, 2) == 1), 1.0, 0.0
    )
    rank_now = count((now_column == now) & (lower < upper), 1)
    rank_next = count((column(later) == later) & (upper < lower), 0)
    turned = upper == lax.rem(lower, N_Z) * N_YC + lower // N_Z
    now_turned = jnp.sum(jnp.where(turned, now_column, 0.0), axis=0, keepdims=True)
    rank_turned = jnp.sum(jnp.where(turned, rank_now, 0.0), axis=0, keepdims=True)
    tall = (ROWS, N_EP)
    row, lane = iota(tall, 0), iota(tall, 1)
    own = lane == lax.rem(row // 2, N_Z) * N_YC + row // (2 * N_Z)
    wanted = jnp.sum(jnp.where(own, later, 0.0), axis=1, keepdims=True)
    leads = jnp.sum(jnp.where(own, rank_next, 0.0), axis=1, keepdims=True) == 0.0
    pair = lax.rem(row, 2).astype(F32)
    to_slot = jnp.where((wanted == named) & (place == pair), 1.0, 0.0)
    back = jnp.where(leads, to_slot, 0.0)
    flag = jnp.sum(to_slot * second, axis=1, keepdims=True)
    hop = jnp.where((wanted == now_turned) & (rank_turned == pair), 1.0, 0.0)
    return to_slot.astype(BF16), back.astype(BF16), flag, hop.astype(BF16)


def kernel(
    og_ref, ha_ref, named_ref, pick_ref, weight_ref, now_ref, next_ref,
    out_ref, mov_ref, upd_ref,
    og_in, ha_in, weight_in, tables, home, moved, updated,
    wb, wz, wp, wide, chosen, pay, hop, w01,
    ogs, ogx, ogy, ogp, ogz, has, hy, hp, hg, back,
    lhs, grad, gram, gram_got, poly, turn,
    part_send, part_got, total, sums, bz, bp, ret,
    wz_sem, wy_sem, hopy_sem, hopz_sem, x_sem, y_sem, z_sem, hy_sem, hz_sem, hx_sem,
    g_sem, a_sem, p_sem, bz_sem, by_sem, in_sem, out_sem,
):
    me = lax.axis_index("ep")
    col = lax.axis_index("dp")
    z = me // N_YC
    yc = lax.rem(me, N_YC)

    def over_z(body):
        def step(k, carry):
            away = jnp.where(lax.rem(k, 2) == 1, (k + 1) // 2, N_Z - k // 2)
            peer = lax.rem(z + away, N_Z)
            body(peer, {"ep": peer * N_YC + yc})
            return carry

        lax.fori_loop(1, N_Z, step, 0)

    def over_yc(body):
        def step(k, carry):
            peer = lax.rem(yc + k, N_YC)
            body(peer, {"ep": z * N_YC + peer})
            return carry

        lax.fori_loop(1, N_YC, step, 0)

    my16, my32z, my32y = span(z * 16, 16), span(z * 32, 32), span(yc * 32, 32)
    my_half, my_cols = span((yc // 4) * 16, 16), span(lax.rem(yc, 4) * 128, 128)

    loads = [(weight_ref, weight_in), (og_ref, og_in), (ha_ref, ha_in)]
    loads += [(r, tables.at[i]) for i, r in enumerate((named_ref, pick_ref, now_ref, next_ref))]
    loads = [pltpu.make_async_copy(*pair, in_sem.at[i]) for i, pair in enumerate(loads)]
    for load in loads:
        load.start()
    chunks = [pl.ds(c * CHUNK, CHUNK) for c in range(CHUNKS)]
    greet(z, yc, col)

    loads[0].wait()
    wb[...] = weight_in[...].astype(BF16)
    pl.semaphore_wait(pltpu.get_barrier_semaphore(), N_Z - 1 + N_YC - 1 + N_DP - 1)
    over_z(lambda peer, there: send(wb.at[span(peer * 32, 32), :], wz.at[z], wz_sem, there))
    wz[z] = wb[my32z, :]

    for load in loads[1:]:
        load.wait()
    to_slot, leading, flag, hop_onehot = plan(*[tables[i] for i in range(4)])
    back[...] = leading
    ogs[...] = pick(to_slot, og_in[...])
    for k in range(1, N_DP):
        peer = lax.rem(col + k, N_DP)
        send(ogs.at[:, span(peer * WIDE, WIDE)], ogx.at[col], x_sem, {"dp": peer})
    has[:, :WIDE] = pick(to_slot, ha_in[...])
    has[:, WIDE:] = jnp.broadcast_to(flag, (ROWS, FLAG)).astype(BF16)
    over_yc(
        lambda peer, there: send(has.at[span(peer * 32, 32), :], hy.at[my32y, :], hy_sem, there)
    )
    hy[my32y, :] = has[my32y, :]
    ogx[col] = ogs[:, span(col * WIDE, WIDE)]

    wait_bytes(hy.at[pl.ds(0, 32 * (N_YC - 1)), :], hy_sem.at[1])
    hp[...] = turn_rows(hy[...], N_Z, N_YC)
    over_z(
        lambda peer, there: send(
            hp.at[span(peer * 16, 16), :], hg.at[col, my16, :], hz_sem, there
        )
    )
    hg[col, my16, :] = hp[my16, :]

    wait_bytes(ogx.at[pl.ds(0, N_DP - 1)], x_sem.at[1])
    over_yc(
        lambda peer, there: send(
            ogx.at[:, span(peer * 32, 32), :], ogy.at[:, my32y, :], y_sem, there
        )
    )
    ogy[:, my32y, :] = ogx[:, my32y, :]

    wait_bytes(wz.at[pl.ds(0, N_Z - 1)], wz_sem.at[1])
    over_yc(
        lambda peer, there: send(
            wz.at[:, span((peer // 4) * 16, 16), span(lax.rem(peer, 4) * 128, 128)],
            wp.at[yc], wy_sem, there,
        )
    )
    wp[yc] = wz[:, my_half, my_cols]

    wait_bytes(ogy.at[:, pl.ds(0, 32 * (N_YC - 1)), :], y_sem.at[1])
    for g in range(N_DP):
        ogp[g] = turn_rows(ogy[g], N_Z, N_YC)
    over_z(
        lambda peer, there: send(
            ogp.at[:, span(peer * 16, 16), :], ogz.at[:, my16, :], z_sem, there
        )
    )
    ogz[:, my16, :] = ogp[:, my16, :]

    wait_bytes(wp.at[pl.ds(0, N_YC - 1)], wy_sem.at[1])
    wide[...] = wp[...].reshape(N_EP * 16, 128).astype(F32)
    for j in range(16):
        piece = wide[pl.ds(j, N_EP, stride=16), :].astype(BF16)
        chosen[pl.ds(j, ROWS, stride=16), :] = jnp.dot(
            hop_onehot, piece, preferred_element_type=F32
        )
    pay[...] = chosen[...].astype(BF16).reshape(N_YC, N_Z, 2, 16, 128)
    over_yc(
        lambda peer, there: send(
            pay.at[peer], hop.at[:, :, my_half, my_cols], hopy_sem, there
        )
    )
    hop[:, :, my_half, my_cols] = pay[yc]

    wait_bytes(hp.at[pl.ds(0, 16 * (N_Z - 1)), :], hz_sem.at[1])
    for k in range(1, N_DP):
        peer = lax.rem(col + k, N_DP)
        send(hg.at[col], hg.at[col], hx_sem, {"dp": peer})

    wait_bytes(pay.at[pl.ds(0, N_YC - 1)], hopy_sem.at[1])
    for lanes, sem in zip(chunks, range(CHUNKS)):
        over_z(
            lambda peer, there: send(
                hop.at[peer, :, :, lanes], w01.at[:, my32z, lanes], hopz_sem.at[sem], there
            )
        )
    w01[:, my32z, :] = hop[z]

    def partials(c):
        wait_bytes(hop.at[pl.ds(0, N_Z - 1), :, :, chunks[c]], hopz_sem.at[c, 1])
        weight = w01[:, :, chunks[c]].reshape(2 * WIDE, CHUNK)
        for k in (1, 2, 3, 0):
            g = lax.rem(col + k, N_DP)
            product = jnp.dot(lhs[g], weight, preferred_element_type=F32)
            if k:
                part_send[c, k - 1] = product.astype(BF16)
                send(part_send.at[c, k - 1], part_got.at[c, k - 1], p_sem.at[c], {"dp": g})
            else:
                total[c] = product

    def add_up(c):
        wait_bytes(part_got.at[c], p_sem.at[c, 1])
        got = part_got[c].astype(F32)
        sums[c] = (total[c] + got[0] + got[1] + got[2]).astype(BF16)

    def home_z(c):
        over_z(
            lambda peer, there: send(
                sums.at[c, span(peer * 16, 16), :], bz.at[c, my16, :], bz_sem.at[c], there
            )
        )
        bz[c, my16, :] = sums[c, my16, :]

    def home_yc(c):
        wait_bytes(bz.at[c, pl.ds(0, 16 * (N_Z - 1)), :], bz_sem.at[c, 1])
        bp[c] = turn_rows(bz[c], N_YC, N_Z)
        over_yc(
            lambda peer, there: send(
                bp.at[c, span(peer * 32, 32), :], ret.at[c, my32y, :], by_sem.at[c], there
            )
        )
        ret[c, my32y, :] = bp[c, my32y, :]

    wait_bytes(hg.at[pl.ds(0, N_DP - 1)], hx_sem.at[1])
    wait_bytes(ogz.at[:, pl.ds(0, 16 * (N_Z - 1)), :], z_sem.at[1])
    acts = hg[:, :, :WIDE].reshape(N_DP * ROWS, WIDE)
    for c in range(0, WIDE, 256):
        grad[c : c + 256, :] = lax.dot_general(
            ogz[:, :, c : c + 256].reshape(N_DP * ROWS, 256),
            acts,
            (((0,), (0,)), ((), ())),
            preferred_element_type=F32,
        )

    for k in (1, 2, 3, 0):
        peer = lax.rem(col + k, N_DP)
        block = span(peer * 128, 128)
        gram[block, :] = exact(grad[:, block].T, grad[...])
        if k:
            send(gram.at[block, :], gram_got.at[k - 1], g_sem.at[k - 1], {"dp": peer})
    for g in range(N_DP):
        second = jnp.concatenate([hg[g, :, WIDE:]] * (WIDE // FLAG), axis=1).astype(F32)
        rows = ogz[g].astype(F32)
        lhs[g, :, :WIDE] = (rows * (1.0 - second)).astype(BF16)
        lhs[g, :, WIDE:] = (rows * second).astype(BF16)
    share = gram[span(col * 128, 128), :]
    for k in range(1, N_DP):
        wait_bytes(gram_got.at[k - 1], g_sem.at[k - 1, 1])
        share = share + gram_got[k - 1]
    poly[span(col * 128, 128), :] = share
    for k in range(1, N_DP):
        peer = lax.rem(col + k, N_DP)
        send(
            poly.at[span(col * 128, 128), :], poly.at[span(col * 128, 128), :], a_sem,
            {"dp": peer},
        )
    for k in range(1, N_DP):
        wait_bytes(gram_got.at[k - 1], g_sem.at[k - 1, 0])
    wait_bytes(gram_got, a_sem.at[1])
    wait_bytes(gram_got, a_sem.at[0])

    eye = jnp.where(iota((WIDE, WIDE), 0) == iota((WIDE, WIDE), 1), 1.0, 0.0)
    square = jnp.sum(poly[...] * eye, keepdims=True)
    scale = 1.0 / (jnp.sqrt(square) + EPSILON)
    a1 = poly[...] * scale * scale
    q1 = POLY_FIRST * eye + POLY_SECOND * a1 + POLY_THIRD * exact(a1, a1)
    a2 = exact(exact(q1, a1), q1)
    q2 = POLY_FIRST * eye + POLY_SECOND * a2 + POLY_THIRD * exact(a2, a2)
    turn[...] = exact(q1, q2) * (scale * (UPDATE_SCALE * (N_DP * WIDE) ** 0.5))
    partials(0)
    updated[...] = exact(grad[...], turn[...])
    save_update = pltpu.make_async_copy(updated, upd_ref, out_sem.at[0])
    save_update.start()

    add_up(0)
    partials(1)
    home_z(0)
    moved[...] = w01[0].astype(F32) - LEARNING_RATE * updated[...]
    save_moved = pltpu.make_async_copy(moved, mov_ref, out_sem.at[1])
    save_moved.start()
    add_up(1)
    home_z(1)
    for c in range(CHUNKS):
        home_yc(c)
    for c in range(CHUNKS):
        wait_bytes(ret.at[c, pl.ds(0, 32 * (N_YC - 1)), :], by_sem.at[c, 1])
        home[:, chunks[c]] = lax.dot_general(
            back[...], ret[c], (((0,), (0,)), ((), ())), preferred_element_type=F32
        )
    save_home = pltpu.make_async_copy(home, out_ref, out_sem.at[2])
    save_home.start()

    for c in range(CHUNKS):
        wait_bytes(part_got.at[c], p_sem.at[c, 0])
        wait_bytes(bz.at[c, pl.ds(0, 16 * (N_Z - 1)), :], bz_sem.at[c, 0])
        wait_bytes(ret.at[c, pl.ds(0, 32 * (N_YC - 1)), :], by_sem.at[c, 0])
    wait_bytes(wz.at[pl.ds(0, N_Z - 1)], wz_sem.at[0])
    wait_bytes(wp.at[pl.ds(0, N_YC - 1)], wy_sem.at[0])
    wait_bytes(pay.at[pl.ds(0, N_YC - 1)], hopy_sem.at[0])
    for c in range(CHUNKS):
        wait_bytes(hop.at[pl.ds(0, N_Z - 1), :, :, chunks[c]], hopz_sem.at[c, 0])
    wait_bytes(ogx.at[pl.ds(0, N_DP - 1)], x_sem.at[0])
    wait_bytes(ogy.at[:, pl.ds(0, 32 * (N_YC - 1)), :], y_sem.at[0])
    wait_bytes(ogz.at[:, pl.ds(0, 16 * (N_Z - 1)), :], z_sem.at[0])
    wait_bytes(hy.at[pl.ds(0, 32 * (N_YC - 1)), :], hy_sem.at[0])
    wait_bytes(hp.at[pl.ds(0, 16 * (N_Z - 1)), :], hz_sem.at[0])
    wait_bytes(hg.at[pl.ds(0, N_DP - 1)], hx_sem.at[0])
    save_update.wait()
    save_moved.wait()
    save_home.wait()


def call(kernel, outs, scratch, semaphores, collective_id, *args):
    hbm = pl.BlockSpec(memory_space=pltpu.HBM)
    return pl.pallas_call(
        kernel,
        out_shape=[jax.ShapeDtypeStruct(*o) for o in outs],
        in_specs=[hbm] * len(args),
        out_specs=[hbm] * len(outs),
        scratch_shapes=[pltpu.VMEM(*s) for s in scratch]
        + [pltpu.SemaphoreType.DMA(s) for s in semaphores],
        compiler_params=pltpu.CompilerParams(
            collective_id=collective_id, has_side_effects=True, vmem_limit_bytes=58 * 2**20
        ),
    )(*args)


def per_device(
    out_grads, hidden_acts, routing, replica_pick, master_weights, current_slots, next_slots
):
    wide_acts = WIDE + FLAG
    input_grads, moved_weight, update = call(
        kernel,
        [((N_EP, WIDE), F32), ((WIDE, WIDE), F32), ((WIDE, WIDE), F32)],
        [
            ((N_EP, N_DP * WIDE), BF16),
            ((N_EP, WIDE), BF16),
            ((WIDE, WIDE), F32),
            ((4, 1, N_EP), jnp.int32),
            ((N_EP, WIDE), F32),
            ((WIDE, WIDE), F32),
            ((WIDE, WIDE), F32),
            ((WIDE, WIDE), BF16),
            ((N_Z, 32, WIDE), BF16),
            ((N_YC, N_Z, 16, 128), BF16),
            ((N_EP * 16, 128), F32),
            ((ROWS * 16, 128), F32),
            ((N_YC, N_Z, 2, 16, 128), BF16),
            ((N_Z, 2, 32, WIDE), BF16),
            ((2, WIDE, WIDE), BF16),
            ((ROWS, N_DP * WIDE), BF16),
            ((N_DP, ROWS, WIDE), BF16),
            ((N_DP, ROWS, WIDE), BF16),
            ((N_DP, ROWS, WIDE), BF16),
            ((N_DP, ROWS, WIDE), BF16),
            ((ROWS, wide_acts), BF16),
            ((ROWS, wide_acts), BF16),
            ((ROWS, wide_acts), BF16),
            ((N_DP, ROWS, wide_acts), BF16),
            ((ROWS, N_EP), BF16),
            ((N_DP, ROWS, 2 * WIDE), BF16),
            ((WIDE, WIDE), F32),
            ((WIDE, WIDE), F32),
            ((3, 128, WIDE), F32),
            ((WIDE, WIDE), F32),
            ((WIDE, WIDE), F32),
            ((CHUNKS, 3, ROWS, CHUNK), BF16),
            ((CHUNKS, 3, ROWS, CHUNK), BF16),
            ((CHUNKS, ROWS, CHUNK), F32),
            ((CHUNKS, ROWS, CHUNK), BF16),
            ((CHUNKS, ROWS, CHUNK), BF16),
            ((CHUNKS, ROWS, CHUNK), BF16),
            ((CHUNKS, ROWS, CHUNK), BF16),
        ],
        [(2,)] * 3 + [(CHUNKS, 2)] + [(2,)] * 6 + [(3, 2), (2,)] + [(CHUNKS, 2)] * 3 + [(7,), (3,)],
        0,
        out_grads,
        hidden_acts,
        routing.reshape(1, N_EP),
        replica_pick.reshape(1, N_EP),
        master_weights[0],
        current_slots.reshape(1, N_EP),
        next_slots.reshape(1, N_EP),
    )
    return (input_grads, moved_weight[None], update[None])


def solution(mesh):
    placed = (
        P(("ep", "dp"), None),
        P(("ep", "dp"), None),
        P(("ep", "dp"), None),
        P(("ep", "dp")),
        P("ep", "dp", None),
        P(),
        P(),
    )
    return jax.shard_map(
        per_device,
        mesh=mesh,
        in_specs=placed,
        out_specs=(P(("ep", "dp"), None), P("ep", "dp", None), P("ep", "dp", None)),
        check_vma=False,
    )
```
